32 devices in a mesh: row: 8 (over z, core), col: 4 (over y, x).
Axes of the slice: x: 2, y: 2, z: 4, core: 2. Of those that a mesh axis runs over, the one named last changes fastest.
Arguments:
- multipliers: float32 [32, 2, 16, 256], P(('row', 'col')), may hold values from -6 to 6
- residual: float32 [32, 2, 16, 256], P(('row', 'col')), may hold values from -18 to 18
- direction: float32 [32, 2, 16, 256], P(('row', 'col')), may hold values from -6 to 6
- energy_prev: float32 [16], replicated, may hold values from 32768 to 131072
- hypersingular: bfloat16 [32, 1152, 1152], P(('row', 'col')), may hold values from -1 to 4, as said below
- double_layer: bfloat16 [32, 1152, 1152], P(('row', 'col')), may hold values from -0.1875 to 0.1875
- single_inverse: bfloat16 [32, 1152, 1152], P(('row', 'col')), may hold values from -1 to 4, as said below
- neumann_inverse: bfloat16 [32, 1152, 1152], P(('row', 'col')), may hold values from -1 to 4, as said below
- rigid_modes: float32 [32, 6, 1152], P(('row', 'col')), may hold values from -0.75 to 0.75
- coarse_inverse: float32 [192, 192], P(('row', 'col')), may hold values from -0.875 to 0.875
- face_index: int32 [32, 4, 256], P(('row', 'col')), may hold values from 0 to 1151, as said below
Outputs:
- multipliers_next: float32 [32, 2, 16, 256], P(('row', 'col'))
- residual_next: float32 [32, 2, 16, 256], P(('row', 'col'))
- direction_next: float32 [32, 2, 16, 256], P(('row', 'col'))
The draws below stay inside these ranges and needn't reach their ends.
Inputs may be any that keep to these rules, and one draw needn't show every extreme that they name: For each patch the 1024 entries of face_index are distinct. `hypersingular`: each patch's matrix is symmetric positive definite. `single_inverse`: each patch's matrix is symmetric positive definite. `neumann_inverse`: each patch's matrix is symmetric positive definite.
All inputs are finite; a program needn't handle non-finite values.
Results may differ from the reference program's by a relative error of at most 0.0015.
Values sent between devices are 32-bit elements; how exact they have to be, the bound alone decides.
A program may use at most 64 MiB of HBM per device.

```python
import math
import jax
import jax.numpy as jnp
from jax import lax

NB = 1152
IF = 256
NRHS = 16
RM = 6
ITERS = 1
PATCHES = 32
N_ROW = 8
N_COL = 4


def symmetric_block(key):

    def one_patch(patch_index):
        sub_key = jax.random.fold_in(key, patch_index)
        key_pair = jax.random.split(sub_key, 2)
        diagonal = jax.random.uniform(key_pair[0], (NB,), jnp.float32, 1.2, 3.0)
        off_diagonal = jnp.clip(jax.random.normal(key_pair[1], (NB, NB), jnp.float32), -4.0, 4.0)
        off_diagonal = (off_diagonal + off_diagonal.T) * (0.4 / jnp.sqrt(2.0 * NB))
        return off_diagonal + jnp.diag(diagonal)
    return lax.map(one_patch, jnp.arange(PATCHES))


def draw_hypersingular(key, part):
    return symmetric_block(jax.random.fold_in(key, 101)).astype(jnp.bfloat16)


def draw_single_inverse(key, part):
    return symmetric_block(jax.random.fold_in(key, 202)).astype(jnp.bfloat16)


def draw_neumann_inverse(key, part):
    return symmetric_block(jax.random.fold_in(key, 303)).astype(jnp.bfloat16)


def draw_residual(key, part):
    key_set = jax.random.split(jax.random.fold_in(key, 404), 1)
    rising = 1.0 + 2.0 * jnp.arange(PATCHES, dtype=jnp.float32) / max(PATCHES - 1, 1)
    shape_all = (PATCHES, 2, NRHS, IF)
    base_draw = jnp.clip(jax.random.normal(key_set[0], shape_all, jnp.float32), -6.0, 6.0)
    return jnp.clip(base_draw * rising[:, None, None, None], -18.0, 18.0)


def draw_face_index(key, part):

    def one_patch(patch_index):
        shuffled = jax.random.permutation(jax.random.fold_in(key, patch_index), NB)
        return shuffled[:4 * IF].reshape(4, IF).astype(jnp.int32)
    return lax.map(one_patch, jnp.arange(PATCHES))


def with_spikes(array, key, source, target, shards_of, factor):
    def block_of(dim):
        return (jnp.arange(array.shape[dim]) // (array.shape[dim] // shards_of)).reshape((-1,) + (1,) * (array.ndim - 1 - dim))

    near = jax.random.permutation(key, shards_of)[block_of(target)]
    other_side = (block_of(target) + shards_of // 2) % shards_of
    return jnp.where((block_of(source) == near) | (block_of(source) == other_side), factor * array, array)


def block_scale(stream_key, extent, cuts, least, high):
    gain = 1.0
    for axis_at, parts in cuts:
        draws = jax.random.uniform(jax.random.fold_in(jax.random.fold_in(stream_key, 6), axis_at), (parts,), jnp.float32, least / len(cuts), high / len(cuts))
        gain = gain * jnp.repeat(jnp.exp(draws), extent[axis_at] // parts).reshape((-1,) + (1,) * (len(extent) - 1 - axis_at))
    return gain


def gaussian(stream_key, extent, scale, bound, shards=(), kind=jnp.bfloat16):
    drawn = scale * jax.random.normal(stream_key, extent, jnp.float32)
    if shards:
        drawn = drawn * block_scale(stream_key, extent, shards, -0.22, 0.18)
    return jnp.clip(drawn, -bound, bound).astype(kind)


def gaussian_with(own_key, dims, scale, reach, shards, heavy, kind=jnp.bfloat16):
    result = scale * jax.random.normal(own_key, dims, jnp.float32)
    if shards:
        result = result * block_scale(own_key, dims, shards, -0.22, 0.18)
    return jnp.clip(with_spikes(result, jax.random.fold_in(own_key, 3), *heavy), -reach, reach).astype(kind)


def setup_inputs(seed: int = 0) -> dict:
    arg_keys = jax.random.split(jax.random.key(seed), 12)
    multipliers = gaussian(arg_keys[0], (PATCHES, 2, NRHS, IF), 1.0, 6.0, ((0, 32),), jnp.float32)
    residual = draw_residual(jax.random.fold_in(arg_keys[11], 71), 0)
    direction = gaussian(arg_keys[2], (PATCHES, 2, NRHS, IF), 1.0, 6.0, ((0, 32),), jnp.float32)
    energy_prev = jnp.clip(jnp.exp(jax.random.uniform(arg_keys[3], (NRHS,), jnp.float32, math.log(32768.0), math.log(131072.0))), 32768.0, 131072.0)
    hypersingular = draw_hypersingular(jax.random.fold_in(arg_keys[11], 71), 0)
    double_layer = gaussian(arg_keys[5], (PATCHES, NB, NB), NB ** -0.5, 0.1875, ((0, 32),))
    single_inverse = draw_single_inverse(jax.random.fold_in(arg_keys[11], 71), 0)
    neumann_inverse = draw_neumann_inverse(jax.random.fold_in(arg_keys[11], 71), 0)
    rigid_modes = gaussian(arg_keys[8], (PATCHES, RM, NB), 64 ** -0.5, 0.75, ((0, 32),), jnp.float32)
    coarse_inverse = gaussian_with(arg_keys[9], (PATCHES * RM, PATCHES * RM), (PATCHES * RM) ** -0.5, 0.875, ((0, 32),), (1, 0, 32, 2.75), jnp.float32)
    face_index = draw_face_index(jax.random.fold_in(arg_keys[11], 71), 0)
    return dict(multipliers=multipliers, residual=residual, direction=direction, energy_prev=energy_prev, hypersingular=hypersingular, double_layer=double_layer, single_inverse=single_inverse, neumann_inverse=neumann_inverse, rigid_modes=rigid_modes, coarse_inverse=coarse_inverse, face_index=face_index)


highest = lax.Precision.HIGHEST


def rolled(vectors, row_step, col_step):
    shaped = vectors.reshape((N_ROW, N_COL) + vectors.shape[1:])
    shaped = jnp.roll(shaped, (row_step, col_step), axis=(0, 1))
    return shaped.reshape(vectors.shape)


def spread_faces(values, face_index):
    from_left = rolled(values[:, 0], 0, 1)
    from_below = rolled(values[:, 1], 1, 0)
    pieces = jnp.concatenate([values[:, 0], values[:, 1], -from_left, -from_below], axis=2)
    flat_index = face_index.reshape(face_index.shape[0], -1)

    def place_one(piece_row, where_row):
        return jnp.zeros((piece_row.shape[0], NB), jnp.float32).at[:, where_row].set(piece_row)

    return jax.vmap(place_one)(pieces, flat_index)


def jump_faces(vectors, face_index):
    flat_index = face_index.reshape(face_index.shape[0], -1)

    def pick_one(row_vec, where_row):
        return jnp.take(row_vec, where_row, axis=1)

    picked = jax.vmap(pick_one)(vectors, flat_index)
    face_width = face_index.shape[2]
    own_right = picked[:, :, :face_width]
    own_upper = picked[:, :, face_width:2 * face_width]
    side_left = picked[:, :, 2 * face_width:3 * face_width]
    side_lower = picked[:, :, 3 * face_width:]
    return jnp.stack([own_right - rolled(side_left, 0, -1), own_upper - rolled(side_lower, -1, 0)], axis=1)


def project(values, face_index, rigid_modes, coarse_inverse):
    spread = spread_faces(values, face_index)
    partial_value = jnp.einsum("pmn,pkn->pmk", rigid_modes, spread, precision=highest)
    stacked = partial_value.reshape(-1, partial_value.shape[2])
    coarse_coef = jnp.dot(coarse_inverse, stacked, precision=highest).reshape(partial_value.shape)
    modes_back = jnp.einsum("pmk,pmn->pkn", coarse_coef, rigid_modes, precision=highest)
    return values - jump_faces(modes_back, face_index)


def dirichlet_patch(operands):
    spread, hypersingular, double_layer, single_inverse = operands
    rounded = spread.astype(jnp.bfloat16)
    lifted = (0.5 * rounded.astype(jnp.float32) + jnp.dot(rounded, double_layer, preferred_element_type=jnp.float32)).astype(jnp.bfloat16)
    weighed = jnp.dot(lifted, single_inverse, preferred_element_type=jnp.float32).astype(jnp.bfloat16)
    applied = jnp.dot(rounded, hypersingular, preferred_element_type=jnp.float32) + 0.5 * weighed.astype(jnp.float32) + lax.dot_general(weighed, double_layer, (((1,), (1,)), ((), ())), preferred_element_type=jnp.float32)
    energy = jnp.sum(rounded.astype(jnp.float32) * applied, axis=1)
    return applied, energy


def neumann_patch(operands):
    rounded, neumann_inverse = operands
    return jnp.dot(rounded, neumann_inverse, preferred_element_type=jnp.float32)


def reference(multipliers, residual, direction, energy_prev, hypersingular, double_layer, single_inverse, neumann_inverse, rigid_modes, coarse_inverse, face_index):
    cases = residual.shape[2]
    for iteration in range(ITERS):
        projected = project(residual, face_index, rigid_modes, coarse_inverse)
        spread_now = spread_faces(projected, face_index)
        applied, energy_parts = lax.map(dirichlet_patch, (spread_now, hypersingular, double_layer, single_inverse))
        energy = jnp.sum(energy_parts, axis=0)
        searched = project(jump_faces(applied, face_index), face_index, rigid_modes, coarse_inverse)
        paired = spread_faces(jnp.concatenate([searched, direction], axis=2), face_index).astype(jnp.bfloat16)
        paired_applied = lax.map(neumann_patch, (paired, neumann_inverse))
        step_ratio = energy / energy_prev
        ratio_col = step_ratio[None, :, None]
        spread_dir = paired[:, :cases].astype(jnp.float32) + ratio_col * paired[:, cases:].astype(jnp.float32)
        applied_dir = paired_applied[:, :cases] + ratio_col * paired_applied[:, cases:]
        curvature = jnp.sum(spread_dir * applied_dir, axis=(0, 2))
        step_size = energy / curvature
        direction = searched + step_ratio[None, None, :, None] * direction
        multipliers = multipliers + step_size[None, None, :, None] * direction
        corrected = project(jump_faces(applied_dir, face_index), face_index, rigid_modes, coarse_inverse)
        residual = residual - step_size[None, None, :, None] * corrected
        energy_prev = energy
    return multipliers, residual, direction
```

```python
import functools

import jax
import jax.numpy as jnp
from jax import lax
from jax.experimental import pallas as pl
from jax.experimental.pallas import tpu as pltpu
from jax.sharding import PartitionSpec as P

MESH = pl.DeviceIdType.MESH
NN = (((1,), (0,)), ((), ()))
NT = (((1,), (1,)), ((), ()))
f32 = jnp.float32
bf16 = jnp.bfloat16
GROUPS = 8
SLOTS = 8


def mul(a, b, dims=NN):
    return lax.dot_general(a, b, dims, preferred_element_type=f32)


def split2(x):
    high = x.astype(bf16)
    return high, (x - high.astype(f32)).astype(bf16)


def mul_exact_right(a, b, dims=NN):
    high, low = split2(a)
    rows = a.shape[0]
    both = mul(jnp.concatenate([high, low], axis=0), b, dims)
    return both[:rows] + both[rows:]


def mul3(a, b, dims=NN):
    b_high, b_low = split2(b)
    return mul_exact_right(a, b_high, dims) + mul(a.astype(bf16), b_low, dims)


def iota(shape, dim):
    return lax.broadcasted_iota(jnp.int32, shape, dim)


def kernel(
    n_row, n_col, modes,
    mult_hbm, res_hbm, dir_hbm, eprev_hbm, hyper_hbm, double_hbm, single_hbm, neumann_hbm,
    rigid_hbm, coarse_hbm, face_hbm,
    mult_out, res_out, dir_out,
    mult, res, direc, eprev, hyper, double, single, neumann, rigid, face,
    coarse_all, res_in, dir_in, modes_own, modes_in, one_hot,
    first_own, first_a, first_msg, first_b,
    own2, gather_a2, msg2, gather_b2,
    own3, gather_a3, msg3, gather_b3,
    faces2, faces2_in, faces3, faces3_in,
    local_sem, send_sem, recv_sem,
):
    row = lax.axis_index("row")
    col = lax.axis_index("col")
    cases, width = res.shape[1], res.shape[2]
    nb = double.shape[0]
    lanes = GROUPS * cases

    def at_row(s):
        return (lax.rem(row + s, n_row), col)

    def at_col(s):
        return (row, lax.rem(col + s, n_col))

    neighbours = [at_col(1), at_row(1), at_col(n_col - 1), at_row(n_row - 1)]

    loads = {}
    for i, (name, src, dst) in enumerate([
        ("face", face_hbm, face), ("rigid", rigid_hbm, rigid), ("res", res_hbm, res),
        ("coarse", coarse_hbm, coarse_all.at[0]), ("direc", dir_hbm, direc),
        ("eprev", eprev_hbm, eprev), ("double", double_hbm, double),
        ("hyper", hyper_hbm, hyper), ("single", single_hbm, single),
        ("neumann", neumann_hbm, neumann), ("mult", mult_hbm, mult),
    ]):
        loads[name] = pltpu.make_async_copy(src, dst, local_sem.at[i])
        loads[name].start()

    barrier = pltpu.get_barrier_semaphore()
    for s in range(1, n_row):
        pl.semaphore_signal(barrier, inc=1, device_id=at_row(s), device_id_type=MESH)
    for s in range(1, n_col):
        pl.semaphore_signal(barrier, inc=1, device_id=at_col(s), device_id_type=MESH)
    pl.semaphore_wait(barrier, n_row + n_col - 2)

    sent = []

    def send(src, dst, device):
        i = len(sent)
        copy = pltpu.make_async_remote_copy(
            src_ref=src, dst_ref=dst, send_sem=send_sem.at[i], recv_sem=recv_sem.at[i],
            device_id=device, device_id_type=MESH,
        )
        copy.start()
        sent.append(copy)
        return copy

    res_moves = [send(res_hbm.at[f], res_in.at[f], neighbours[f]) for f in range(2)]
    coarse_moves = [
        send(coarse_hbm, coarse_all.at[1 + (f + 2) % 4], neighbours[f]) for f in range(4)
    ]
    dir_moves = [send(dir_hbm.at[f], dir_in.at[f], neighbours[f]) for f in range(2)]

    loads["face"].wait()
    here = iota((nb, width), 0)
    for f in range(4):
        one_hot[:, f * width:(f + 1) * width] = jnp.where(
            here == face[f:f + 1, :], 1.0, 0.0
        ).astype(bf16)

    loads["rigid"].wait()
    rigid_pad = jnp.concatenate([rigid[...], jnp.zeros((8 - modes, nb), f32)], axis=0)
    modes_face = mul_exact_right(rigid_pad, one_hot[...])
    for f in range(4):
        modes_own[f] = modes_face[:, f * width:(f + 1) * width]
    mode_moves = [
        send(modes_own.at[f], modes_in.at[(f + 2) % 4], neighbours[f]) for f in range(4)
    ]

    lane_at = iota((SLOTS, lanes), 1)
    slot_at = iota((SLOTS, lanes), 0)

    loads["res"].wait()
    for move in res_moves:
        move.wait_recv()
    pieces = jnp.concatenate([res[0], res[1], -res_in[0], -res_in[1]], axis=1)
    g_own = mul3(modes_face, jnp.concatenate([pieces] * GROUPS, axis=0), NT)
    in_group = (lane_at >= slot_at * cases) & (lane_at < (slot_at + 1) * cases)
    first = jnp.sum(jnp.where(in_group, g_own, 0.0), axis=0, keepdims=True)

    def start_rows(message, own, target):
        own[...] = message
        moves = [send(own, target.at[row], at_row(s)) for s in range(1, n_row)]
        target[row] = message
        return moves

    def start_cols(message, own, target):
        own[...] = message
        moves = [send(own, target.at[col], at_col(s)) for s in range(1, n_col)]
        target[col] = message
        return moves

    def finish(moves):
        for move in moves:
            move.wait_recv()

    moves = start_rows(first, first_own, first_a)

    loads["coarse"].wait()
    finish(coarse_moves)
    patches = n_row * n_col
    span = modes * patches
    slot_c = iota((SLOTS, span), 0)
    blocks = []
    for m in range(modes):
        block = jnp.zeros((SLOTS, span), f32)
        for k in range(5):
            block = jnp.where(slot_c == k, coarse_all[k, m:m + 1, :], block)
        blocks.append(block)
    blocks.append(jnp.zeros((lanes - SLOTS * modes, span), f32))
    coarse_rows = jnp.concatenate(blocks, axis=0)
    r_at = iota((n_row, span), 0)
    q_at = iota((n_row, span), 1)
    picks = []
    for j in range(modes):
        for c in range(n_col):
            picks.append(jnp.where(q_at == (r_at * n_col + c) * modes + j, 1.0, 0.0))
    pick = jnp.concatenate(picks, axis=0).astype(bf16)
    coarse_high, coarse_low = split2(coarse_rows)
    solve_high = mul(pick, coarse_high, NT).astype(bf16)
    solve_low = mul(pick, coarse_low, NT).astype(bf16)

    finish(moves)
    moves = start_cols(first_a[:, 0, :], first_msg, first_b)

    finish(mode_moves)
    slot_w = iota((SLOTS, width), 0)
    columns = []
    for f in range(4):
        blocks = []
        for m in range(modes):
            block = jnp.where(slot_w == 0, modes_own[f, m:m + 1, :], 0.0)
            blocks.append(jnp.where(slot_w == 1 + f, -modes_in[f, m:m + 1, :], block))
        columns.append(jnp.concatenate(blocks, axis=0))
    basis = jnp.concatenate(columns, axis=1)
    basis_high, basis_low = split2(basis)
    basis_dof = mul(basis_high, one_hot[...], NT) + mul(basis_low, one_hot[...], NT)
    loads["double"].wait()
    basis_double = 0.5 * basis_dof + mul_exact_right(basis_dof, double[...])

    def correction(g):
        g_t = g.T
        total = jnp.zeros((cases, lanes), f32)
        for j in range(modes):
            rows = slice(j * patches, (j + 1) * patches)
            part = g_t[j * cases:(j + 1) * cases, :]
            total = total + mul_exact_right(part, solve_high[rows])
            total = total + mul(part.astype(bf16), solve_low[rows])
        coef = total[:, :SLOTS * modes]
        return mul_exact_right(coef, basis_high) + mul(coef.astype(bf16), basis_low)

    def message_of(out, scalars):
        message = jnp.zeros((SLOTS, lanes), f32)
        for j in range(modes):
            mask = (lane_at >= j * cases) & (lane_at < (j + 1) * cases)
            message = jnp.where(mask, out[j * SLOTS:(j + 1) * SLOTS], message)
        lane_c = iota((cases, lanes), 1)
        case_c = iota((cases, lanes), 0)
        line = jnp.sum(
            jnp.where(lane_c == case_c + modes * cases, scalars, 0.0), axis=0, keepdims=True
        )
        return message + jnp.where(slot_at == 0, line, 0.0)

    def rolled(x, step):
        step = step % n_row
        return jnp.concatenate([x[n_row - step:], x[:n_row - step]], axis=0)

    def along_rows(buffer):
        own = buffer[:, 0, :] + rolled(buffer[:, 2, :], 1) + rolled(buffer[:, 4, :], -1)
        return jnp.stack([own, buffer[:, 1, :], buffer[:, 3, :]], axis=0)

    def along_cols(buffer):
        tiles = []
        for c in range(n_col):
            tiles.append(
                buffer[c, 0] + buffer[(c - 1) % n_col, 1] + buffer[(c + 1) % n_col, 2]
            )
        return jnp.concatenate(tiles, axis=0)

    def scalars_of(g):
        line = jnp.sum(g, axis=0, keepdims=True)
        lane_c = iota((cases, lanes), 1)
        case_c = iota((cases, lanes), 0)
        return jnp.sum(
            jnp.where(lane_c == case_c + modes * cases, line, 0.0), axis=1, keepdims=True
        )

    def repeated(x):
        return jnp.concatenate([x] * GROUPS, axis=0)

    finish(moves)
    g = jnp.concatenate([first_b[c] for c in range(n_col)], axis=0)
    rounded_faces = (pieces - correction(g)).astype(bf16)
    rounded_full = mul(rounded_faces, one_hot[...], NT)
    rounded = rounded_full.astype(bf16)
    lifted_full = 0.5 * rounded_full + mul(rounded, double[...])
    loads["single"].wait()
    weighed_full = mul(lifted_full.astype(bf16), single[...])
    weighed = weighed_full.astype(bf16)
    weighed_full = weighed.astype(f32)
    loads["hyper"].wait()
    applied = mul(rounded, hyper[...])
    energy_parts = jnp.sum(
        rounded_full * applied + weighed_full * lifted_full, axis=1, keepdims=True
    )
    out = mul3(basis_dof, repeated(applied), NT)
    out = out + mul_exact_right(basis_double, repeated(weighed), NT)
    moves = start_rows(message_of(out, energy_parts), own2, gather_a2)

    applied = applied + 0.5 * weighed_full + mul(weighed, double[...], NT)
    finish(moves)
    moves = start_cols(along_rows(gather_a2), msg2, gather_b2)

    applied_faces = mul_exact_right(applied, one_hot[...])
    for f in range(4):
        faces2[f] = applied_faces[:, f * width:(f + 1) * width]
    face_moves = [
        send(faces2.at[f], faces2_in.at[(f + 2) % 4], neighbours[f]) for f in range(4)
    ]
    loads["direc"].wait()
    finish(dir_moves)
    old_faces = jnp.concatenate([direc[0], direc[1], -dir_in[0], -dir_in[1]], axis=1)
    old_full = mul(old_faces.astype(bf16), one_hot[...], NT)
    loads["neumann"].wait()
    old_applied = mul(old_full.astype(bf16), neumann[...])
    loads["eprev"].wait()
    lane_e = iota((cases, cases), 1)
    case_e = iota((cases, cases), 0)
    energy_prev = jnp.sum(
        jnp.where(lane_e == case_e, eprev[...], 0.0), axis=1, keepdims=True
    )

    finish(face_moves)
    finish(moves)
    g = along_cols(gather_b2)
    energy = scalars_of(g)
    ratio = energy / energy_prev
    jumped = applied_faces - jnp.concatenate([faces2_in[f] for f in range(4)], axis=1)
    searched = jumped - correction(g)
    new_full = mul(searched.astype(bf16), one_hot[...], NT)
    new_applied = mul(new_full.astype(bf16), neumann[...])
    spread_dir = new_full + ratio * old_full
    applied_dir = new_applied + ratio * old_applied
    curvature_parts = jnp.sum(spread_dir * applied_dir, axis=1, keepdims=True)
    out = mul3(basis_dof, repeated(applied_dir), NT)
    moves = start_rows(message_of(out, curvature_parts), own3, gather_a3)
    dir_faces = mul_exact_right(applied_dir, one_hot[...])
    for f in range(2):
        faces3[f] = dir_faces[:, (f + 2) * width:(f + 3) * width]
    face_moves = [send(faces3.at[f], faces3_in.at[f], neighbours[f + 2]) for f in range(2)]
    finish(moves)
    moves = start_cols(along_rows(gather_a3), msg3, gather_b3)
    loads["mult"].wait()
    next_dir = [
        searched[:, f * width:(f + 1) * width] + ratio * direc[f] for f in range(2)
    ]
    for f in range(2):
        dir_out[f] = next_dir[f]
    finish(face_moves)
    finish(moves)
    g = along_cols(gather_b3)
    step = energy / scalars_of(g)
    fix = correction(g)
    for f in range(2):
        part = slice(f * width, (f + 1) * width)
        mult_out[f] = mult[f] + step * next_dir[f]
        res_out[f] = res[f] - step * (dir_faces[:, part] - faces3_in[f] - fix[:, part])

    for copy in sent:
        copy.wait_send()


def on_device(
    multipliers, residual, direction, energy_prev, hypersingular, double_layer,
    single_inverse, neumann_inverse, rigid_modes, coarse_inverse, face_index,
):
    n_row, n_col = lax.axis_size("row"), lax.axis_size("col")
    _, sides, cases, width = residual.shape
    modes, nb = rigid_modes.shape[1:]
    lanes = GROUPS * cases
    values = jax.ShapeDtypeStruct((sides, cases, width), f32)
    matrix = pltpu.VMEM((nb, nb), bf16)
    copies = 12 + 3 * (n_row + n_col - 2) + 6

    def vmem(*shape):
        return pltpu.VMEM(shape, f32)

    outs = pl.pallas_call(
        functools.partial(kernel, n_row, n_col, modes),
        out_shape=(values, values, values),
        in_specs=[pl.BlockSpec(memory_space=pl.ANY)] * 11,
        out_specs=[pl.BlockSpec(memory_space=pltpu.VMEM)] * 3,
        scratch_shapes=[
            vmem(sides, cases, width), vmem(sides, cases, width), vmem(sides, cases, width),
            vmem(1, cases), matrix, matrix, matrix, matrix,
            vmem(modes, nb), pltpu.VMEM(face_index.shape[1:], jnp.int32),
            vmem(5, *coarse_inverse.shape), vmem(2, cases, width), vmem(2, cases, width),
            vmem(4, 8, width), vmem(4, 8, width), pltpu.VMEM((nb, 4 * width), bf16),
            vmem(1, lanes), vmem(n_row, 1, lanes), vmem(n_row, lanes), vmem(n_col, n_row, lanes),
            vmem(SLOTS, lanes), vmem(n_row, SLOTS, lanes),
            vmem(3, n_row, lanes), vmem(n_col, 3, n_row, lanes),
            vmem(SLOTS, lanes), vmem(n_row, SLOTS, lanes),
            vmem(3, n_row, lanes), vmem(n_col, 3, n_row, lanes),
            vmem(4, cases, width), vmem(4, cases, width),
            vmem(2, cases, width), vmem(2, cases, width),
            pltpu.SemaphoreType.DMA((11,)),
            pltpu.SemaphoreType.DMA((copies,)),
            pltpu.SemaphoreType.DMA((copies,)),
        ],
        compiler_params=pltpu.CompilerParams(
            collective_id=0, has_side_effects=True, vmem_limit_bytes=48 * 1024 * 1024
        ),
        cost_estimate=pl.CostEstimate(
            flops=40 * cases * nb * nb, bytes_accessed=8 * nb * nb, transcendentals=0
        ),
    )(
        multipliers[0], residual[0], direction[0], energy_prev.reshape(1, cases),
        hypersingular[0], double_layer[0], single_inverse[0], neumann_inverse[0],
        rigid_modes[0], coarse_inverse, face_index[0],
    )
    return tuple(out[None] for out in outs)


def solution(mesh):
    split = ("row", "col")
    faces = P(split, None, None, None)
    cube = P(split, None, None)
    return jax.shard_map(
        on_device,
        mesh=mesh,
        in_specs=(
            faces, faces, faces, P(), cube, cube, cube, cube, cube, P(split, None), cube,
        ),
        out_specs=(faces, faces, faces),
        check_vma=False,
    )
```

```python
import functools

import jax
import jax.numpy as jnp
from jax import lax
from jax.experimental import pallas as pl
from jax.experimental.pallas import tpu as pltpu
from jax.sharding import PartitionSpec as P

MESH = pl.DeviceIdType.MESH
NN = (((1,), (0,)), ((), ()))
NT = (((1,), (1,)), ((), ()))
f32 = jnp.float32
bf16 = jnp.bfloat16
GROUPS = 8
SLOTS = 8


def mul(a, b, dims=NN):
    return lax.dot_general(a, b, dims, preferred_element_type=f32)


def split2(x):
    high = x.astype(bf16)
    return high, (x - high.astype(f32)).astype(bf16)


def mul_exact_right(a, b, dims=NN):
    high, low = split2(a)
    rows = a.shape[0]
    both = mul(jnp.concatenate([high, low], axis=0), b, dims)
    return both[:rows] + both[rows:]


def mul3(a, b, dims=NN):
    b_high, b_low = split2(b)
    return mul_exact_right(a, b_high, dims) + mul(a.astype(bf16), b_low, dims)


def iota(shape, dim):
    return lax.broadcasted_iota(jnp.int32, shape, dim)


def kernel(
    n_row, n_col, modes,
    res_hbm, dir_hbm, eprev_hbm, hyper_hbm, double_hbm, single_hbm, neumann_hbm,
    rigid_hbm, coarse_hbm, face_hbm,
    out_ref,
    res, direc, eprev, hyper, double, single, neumann, rigid, face,
    coarse_all, res_in, dir_in, modes_own, modes_in, one_hot,
    first_own, first_a, first_msg, first_b,
    own2, gather_a2, msg2, gather_b2,
    own3, gather_a3, msg3, gather_b3,
    faces2, faces2_in, faces3, faces3_in,
    local_sem, send_sem, recv_sem,
):
    row = lax.axis_index("row")
    col = lax.axis_index("col")
    cases, width = res.shape[1], res.shape[2]
    nb = double.shape[0]
    lanes = GROUPS * cases

    def at_row(s):
        return (lax.rem(row + s, n_row), col)

    def at_col(s):
        return (row, lax.rem(col + s, n_col))

    neighbours = [at_col(1), at_row(1), at_col(n_col - 1), at_row(n_row - 1)]

    loads = {}
    for i, (name, src, dst) in enumerate([
        ("face", face_hbm, face), ("rigid", rigid_hbm, rigid), ("res", res_hbm, res),
        ("coarse", coarse_hbm, coarse_all.at[0]), ("direc", dir_hbm, direc),
        ("eprev", eprev_hbm, eprev), ("double", double_hbm, double),
        ("hyper", hyper_hbm, hyper), ("single", single_hbm, single),
        ("neumann", neumann_hbm, neumann),
    ]):
        loads[name] = pltpu.make_async_copy(src, dst, local_sem.at[i])
        loads[name].start()

    barrier = pltpu.get_barrier_semaphore()
    for s in range(1, n_row):
        pl.semaphore_signal(barrier, inc=1, device_id=at_row(s), device_id_type=MESH)
    for s in range(1, n_col):
        pl.semaphore_signal(barrier, inc=1, device_id=at_col(s), device_id_type=MESH)
    pl.semaphore_wait(barrier, n_row + n_col - 2)

    sent = []

    def send(src, dst, device):
        i = len(sent)
        copy = pltpu.make_async_remote_copy(
            src_ref=src, dst_ref=dst, send_sem=send_sem.at[i], recv_sem=recv_sem.at[i],
            device_id=device, device_id_type=MESH,
        )
        copy.start()
        sent.append(copy)
        return copy

    res_moves = [send(res_hbm.at[f], res_in.at[f], neighbours[f]) for f in range(2)]
    coarse_moves = [
        send(coarse_hbm, coarse_all.at[1 + (f + 2) % 4], neighbours[f]) for f in range(4)
    ]
    dir_moves = [send(dir_hbm.at[f], dir_in.at[f], neighbours[f]) for f in range(2)]

    loads["face"].wait()
    here = iota((nb, width), 0)
    for f in range(4):
        one_hot[:, f * width:(f + 1) * width] = jnp.where(
            here == face[f:f + 1, :], 1.0, 0.0
        ).astype(bf16)

    loads["rigid"].wait()
    rigid_pad = jnp.concatenate(
        [rigid[m] for m in range(modes)] + [jnp.zeros((8 - modes, nb), f32)], axis=0
    )
    modes_face = mul_exact_right(rigid_pad, one_hot[...])
    for f in range(4):
        modes_own[f] = modes_face[:, f * width:(f + 1) * width]
    mode_moves = [
        send(modes_own.at[f], modes_in.at[(f + 2) % 4], neighbours[f]) for f in range(4)
    ]

    lane_at = iota((SLOTS, lanes), 1)
    slot_at = iota((SLOTS, lanes), 0)

    loads["res"].wait()
    for move in res_moves:
        move.wait_recv()
    pieces = jnp.concatenate([res[0], res[1], -res_in[0], -res_in[1]], axis=1)
    g_own = mul3(modes_face, jnp.concatenate([pieces] * GROUPS, axis=0), NT)
    in_group = (lane_at >= slot_at * cases) & (lane_at < (slot_at + 1) * cases)
    first = jnp.sum(jnp.where(in_group, g_own, 0.0), axis=0, keepdims=True)

    def start_rows(message, own, target):
        own[...] = message
        moves = [send(own, target.at[row], at_row(s)) for s in range(1, n_row)]
        target[row] = message
        return moves

    def start_cols(message, own, target):
        own[...] = message
        moves = [send(own, target.at[col], at_col(s)) for s in range(1, n_col)]
        target[col] = message
        return moves

    def finish(moves):
        for move in moves:
            move.wait_recv()

    moves = start_rows(first, first_own, first_a)

    loads["coarse"].wait()
    finish(coarse_moves)
    patches = n_row * n_col
    span = modes * patches
    slot_c = iota((SLOTS, span), 0)
    blocks = []
    for m in range(modes):
        block = jnp.zeros((SLOTS, span), f32)
        for k in range(5):
            block = jnp.where(slot_c == k, coarse_all[k, m:m + 1, :], block)
        blocks.append(block)
    blocks.append(jnp.zeros((lanes - SLOTS * modes, span), f32))
    coarse_rows = jnp.concatenate(blocks, axis=0)
    r_at = iota((n_row, span), 0)
    q_at = iota((n_row, span), 1)
    picks = []
    for j in range(modes):
        for c in range(n_col):
            picks.append(jnp.where(q_at == (r_at * n_col + c) * modes + j, 1.0, 0.0))
    pick = jnp.concatenate(picks, axis=0).astype(bf16)
    coarse_high, coarse_low = split2(coarse_rows)
    solve_high = mul(pick, coarse_high, NT).astype(bf16)
    solve_low = mul(pick, coarse_low, NT).astype(bf16)

    finish(moves)
    moves = start_cols(first_a[:, 0, :], first_msg, first_b)

    finish(mode_moves)
    slot_w = iota((SLOTS, width), 0)
    columns = []
    for f in range(4):
        blocks = []
        for m in range(modes):
            block = jnp.where(slot_w == 0, modes_own[f, m:m + 1, :], 0.0)
            blocks.append(jnp.where(slot_w == 1 + f, -modes_in[f, m:m + 1, :], block))
        columns.append(jnp.concatenate(blocks, axis=0))
    basis = jnp.concatenate(columns, axis=1)
    basis_high, basis_low = split2(basis)
    basis_dof = mul_exact_right(basis, one_hot[...], NT)
    loads["double"].wait()
    basis_double = 0.5 * basis_dof + mul_exact_right(basis_dof, double[...])

    def correction(g):
        g_t = g.T
        total = jnp.zeros((cases, lanes), f32)
        for j in range(modes):
            rows = slice(j * patches, (j + 1) * patches)
            part = g_t[j * cases:(j + 1) * cases, :]
            total = total + mul_exact_right(part, solve_high[rows])
            total = total + mul(part.astype(bf16), solve_low[rows])
        coef = total[:, :SLOTS * modes]
        return mul_exact_right(coef, basis_high) + mul(coef.astype(bf16), basis_low)

    def message_of(out, scalars):
        message = jnp.zeros((SLOTS, lanes), f32)
        for j in range(modes):
            mask = (lane_at >= j * cases) & (lane_at < (j + 1) * cases)
            message = jnp.where(mask, out[j * SLOTS:(j + 1) * SLOTS], message)
        lane_c = iota((cases, lanes), 1)
        case_c = iota((cases, lanes), 0)
        line = jnp.sum(
            jnp.where(lane_c == case_c + modes * cases, scalars, 0.0), axis=0, keepdims=True
        )
        return message + jnp.where(slot_at == 0, line, 0.0)

    def rolled(x, step):
        step = step % n_row
        return jnp.concatenate([x[n_row - step:], x[:n_row - step]], axis=0)

    def along_rows(buffer):
        own = buffer[:, 0, :] + rolled(buffer[:, 2, :], 1) + rolled(buffer[:, 4, :], -1)
        return jnp.stack([own, buffer[:, 1, :], buffer[:, 3, :]], axis=0)

    def along_cols(buffer):
        tiles = []
        for c in range(n_col):
            tiles.append(
                buffer[c, 0] + buffer[(c - 1) % n_col, 1] + buffer[(c + 1) % n_col, 2]
            )
        return jnp.concatenate(tiles, axis=0)

    def scalars_of(g):
        line = jnp.sum(g, axis=0, keepdims=True)
        lane_c = iota((cases, lanes), 1)
        case_c = iota((cases, lanes), 0)
        return jnp.sum(
            jnp.where(lane_c == case_c + modes * cases, line, 0.0), axis=1, keepdims=True
        )

    def repeated(x):
        return jnp.concatenate([x] * GROUPS, axis=0)

    finish(moves)
    g = jnp.concatenate([first_b[c] for c in range(n_col)], axis=0)
    rounded_faces = (pieces - correction(g)).astype(bf16)
    rounded_full = mul(rounded_faces, one_hot[...], NT)
    rounded = rounded_full.astype(bf16)
    lifted_full = 0.5 * rounded_full + mul(rounded, double[...])
    loads["single"].wait()
    weighed_full = mul(lifted_full.astype(bf16), single[...])
    weighed = weighed_full.astype(bf16)
    weighed_full = weighed.astype(f32)
    loads["hyper"].wait()
    applied = mul(rounded, hyper[...])
    energy_parts = jnp.sum(
        rounded_full * applied + weighed_full * lifted_full, axis=1, keepdims=True
    )
    out = mul3(basis_dof, repeated(applied), NT)
    out = out + mul_exact_right(basis_double, repeated(weighed), NT)
    moves = start_rows(message_of(out, energy_parts), own2, gather_a2)

    applied = applied + 0.5 * weighed_full + mul(weighed, double[...], NT)
    finish(moves)
    moves = start_cols(along_rows(gather_a2), msg2, gather_b2)

    applied_faces = mul_exact_right(applied, one_hot[...])
    for f in range(4):
        faces2[f] = applied_faces[:, f * width:(f + 1) * width]
    face_moves = [
        send(faces2.at[f], faces2_in.at[(f + 2) % 4], neighbours[f]) for f in range(4)
    ]
    loads["direc"].wait()
    finish(dir_moves)
    old_faces = jnp.concatenate([direc[0], direc[1], -dir_in[0], -dir_in[1]], axis=1)
    old_faces = old_faces.astype(bf16)
    loads["neumann"].wait()
    loads["eprev"].wait()
    lane_e = iota((cases, cases), 1)
    case_e = iota((cases, cases), 0)
    energy_prev = jnp.sum(
        jnp.where(lane_e == case_e, eprev[...], 0.0), axis=1, keepdims=True
    )

    finish(face_moves)
    finish(moves)
    g = along_cols(gather_b2)
    energy = scalars_of(g)
    ratio = energy / energy_prev
    jumped = applied_faces - jnp.concatenate([faces2_in[f] for f in range(4)], axis=1)
    searched = jumped - correction(g)
    paired = jnp.concatenate([searched.astype(bf16), old_faces], axis=0)
    paired = mul(paired, one_hot[...], NT)
    paired_applied = mul(paired.astype(bf16), neumann[...])
    spread_dir = paired[:cases] + ratio * paired[cases:]
    applied_dir = paired_applied[:cases] + ratio * paired_applied[cases:]
    curvature_parts = jnp.sum(spread_dir * applied_dir, axis=1, keepdims=True)
    out = mul3(basis_dof, repeated(applied_dir), NT)
    moves = start_rows(message_of(out, curvature_parts), own3, gather_a3)
    dir_faces = mul_exact_right(applied_dir, one_hot[...])
    for f in range(2):
        faces3[f] = dir_faces[:, (f + 2) * width:(f + 3) * width]
    face_moves = [send(faces3.at[f], faces3_in.at[f], neighbours[f + 2]) for f in range(2)]
    finish(moves)
    moves = start_cols(along_rows(gather_a3), msg3, gather_b3)
    next_dir = [
        searched[:, f * width:(f + 1) * width] + ratio * direc[f] for f in range(2)
    ]
    for f in range(2):
        out_ref[2, f] = searched[:, f * width:(f + 1) * width]
        out_ref[3, f] = ratio * direc[f]
    finish(face_moves)
    finish(moves)
    g = along_cols(gather_b3)
    step = energy / scalars_of(g)
    fix = correction(g)
    for f in range(2):
        part = slice(f * width, (f + 1) * width)
        out_ref[0, f] = step * next_dir[f]
        out_ref[1, f] = step * (dir_faces[:, part] - faces3_in[f] - fix[:, part])

    for copy in sent:
        copy.wait_send()


def on_device(
    multipliers, residual, direction, energy_prev, hypersingular, double_layer,
    single_inverse, neumann_inverse, rigid_modes, coarse_inverse, face_index,
):
    n_row, n_col = lax.axis_size("row"), lax.axis_size("col")
    _, sides, cases, width = residual.shape
    modes, nb = rigid_modes.shape[1:]
    lanes = GROUPS * cases
    matrix = pltpu.VMEM((nb, nb), bf16)
    copies = 12 + 3 * (n_row + n_col - 2) + 6

    def vmem(*shape):
        return pltpu.VMEM(shape, f32)

    out = pl.pallas_call(
        functools.partial(kernel, n_row, n_col, modes),
        out_shape=jax.ShapeDtypeStruct((4, sides, cases, width), f32),
        in_specs=[pl.BlockSpec(memory_space=pltpu.HBM)] * 10,
        out_specs=pl.BlockSpec(memory_space=pltpu.VMEM),
        scratch_shapes=[
            vmem(sides, cases, width), vmem(sides, cases, width),
            vmem(1, cases), matrix, matrix, matrix, matrix,
            vmem(modes, 1, nb), pltpu.VMEM(face_index.shape[1:], jnp.int32),
            vmem(5, *coarse_inverse.shape), vmem(2, cases, width), vmem(2, cases, width),
            vmem(4, 8, width), vmem(4, 8, width), pltpu.VMEM((nb, 4 * width), bf16),
            vmem(1, lanes), vmem(n_row, 1, lanes), vmem(n_row, lanes), vmem(n_col, n_row, lanes),
            vmem(SLOTS, lanes), vmem(n_row, SLOTS, lanes),
            vmem(3, n_row, lanes), vmem(n_col, 3, n_row, lanes),
            vmem(SLOTS, lanes), vmem(n_row, SLOTS, lanes),
            vmem(3, n_row, lanes), vmem(n_col, 3, n_row, lanes),
            vmem(4, cases, width), vmem(4, cases, width),
            vmem(2, cases, width), vmem(2, cases, width),
            pltpu.SemaphoreType.DMA((10,)),
            pltpu.SemaphoreType.DMA((copies,)),
            pltpu.SemaphoreType.DMA((copies,)),
        ],
        compiler_params=pltpu.CompilerParams(
            collective_id=0, has_side_effects=True, vmem_limit_bytes=63 * 1024 * 1024
        ),
        cost_estimate=pl.CostEstimate(
            flops=40 * cases * nb * nb, bytes_accessed=8 * nb * nb, transcendentals=0
        ),
    )(
        residual[0], direction[0], energy_prev.reshape(1, cases),
        hypersingular[0], double_layer[0], single_inverse[0], neumann_inverse[0],
        rigid_modes.transpose(1, 0, 2), coarse_inverse, face_index[0],
    )
    return (multipliers + out[0], residual - out[1], (out[2] + out[3])[None])


def solution(mesh):
    split = ("row", "col")
    faces = P(split, None, None, None)
    cube = P(split, None, None)
    return jax.shard_map(
        on_device,
        mesh=mesh,
        in_specs=(
            faces, faces, faces, P(), cube, cube, cube, cube, cube, P(split, None), cube,
        ),
        out_specs=(faces, faces, faces),
        check_vma=False,
    )
```

```python
import functools

import jax
import jax.numpy as jnp
from jax import lax
from jax.experimental import pallas as pl
from jax.experimental.pallas import tpu as pltpu
from jax.sharding import PartitionSpec as P

MESH = pl.DeviceIdType.MESH
NN = (((1,), (0,)), ((), ()))
NT = (((1,), (1,)), ((), ()))
f32 = jnp.float32
bf16 = jnp.bfloat16
GROUPS = 8
SLOTS = 8


def mul(a, b, dims=NN):
    return lax.dot_general(a, b, dims, preferred_element_type=f32)


def split2(x):
    high = x.astype(bf16)
    return high, (x - high.astype(f32)).astype(bf16)


def mul_exact_right(a, b, dims=NN):
    high, low = split2(a)
    rows = a.shape[0]
    both = mul(jnp.concatenate([high, low], axis=0), b, dims)
    return both[:rows] + both[rows:]


def iota(shape, dim):
    return lax.broadcasted_iota(jnp.int32, shape, dim)


def kernel(
    n_row, n_col, modes,
    res_hbm, dir_hbm, eprev_hbm, hyper_hbm, double_hbm, single_hbm, neumann_hbm,
    rigid_hbm, coarse_hbm, face_hbm,
    out_ref,
    res, direc, eprev, hyper, double, single, neumann, rigid, face,
    coarse_all, res_in, dir_in, modes_own, modes_in, one_hot,
    first_own, first_a, first_msg, first_b,
    own2, gather_a2, msg2, gather_b2,
    own3, gather_a3, msg3, gather_b3,
    faces2, faces2_in, faces3, faces3_in,
    local_sem, send_sem, recv_sem,
):
    row = lax.axis_index("row")
    col = lax.axis_index("col")
    cases, width = res.shape[1], res.shape[2]
    nb = double.shape[0]
    lanes = GROUPS * cases

    def repeated(x):
        return jnp.concatenate([x] * GROUPS, axis=0)

    def at_row(s):
        return (lax.rem(row + s, n_row), col)

    def at_col(s):
        return (row, lax.rem(col + s, n_col))

    neighbours = [at_col(1), at_row(1), at_col(n_col - 1), at_row(n_row - 1)]

    loads = {}

    def load(name, src, dst):
        loads[name] = pltpu.make_async_copy(src, dst, local_sem.at[len(loads)])
        loads[name].start()

    load("face", face_hbm, face)
    load("rigid", rigid_hbm, rigid)
    load("res", res_hbm, res)
    load("coarse", coarse_hbm, coarse_all.at[0])
    load("direc", dir_hbm, direc)
    load("eprev", eprev_hbm, eprev)

    barrier = pltpu.get_barrier_semaphore()
    for s in range(1, n_row):
        pl.semaphore_signal(barrier, inc=1, device_id=at_row(s), device_id_type=MESH)
    for s in range(1, n_col):
        pl.semaphore_signal(barrier, inc=1, device_id=at_col(s), device_id_type=MESH)
    pl.semaphore_wait(barrier, n_row + n_col - 2)

    sent = []

    def send(src, dst, device):
        i = len(sent)
        copy = pltpu.make_async_remote_copy(
            src_ref=src, dst_ref=dst, send_sem=send_sem.at[i], recv_sem=recv_sem.at[i],
            device_id=device, device_id_type=MESH,
        )
        copy.start()
        sent.append(copy)
        return copy

    res_moves = [send(res_hbm.at[f], res_in.at[f], neighbours[f]) for f in range(2)]
    coarse_moves = [
        send(coarse_hbm, coarse_all.at[1 + (f + 2) % 4], neighbours[f]) for f in range(4)
    ]
    dir_moves = [send(dir_hbm.at[f], dir_in.at[f], neighbours[f]) for f in range(2)]
    load("double", double_hbm, double)
    load("single", single_hbm, single)
    load("hyper", hyper_hbm, hyper)
    load("neumann", neumann_hbm, neumann)

    loads["face"].wait()
    here = iota((nb, width), 0)
    for f in range(4):
        one_hot[:, f * width:(f + 1) * width] = jnp.where(
            here == face[f:f + 1, :], 1.0, 0.0
        ).astype(bf16)

    loads["rigid"].wait()
    rigid_pad = jnp.concatenate(
        [rigid[m] for m in range(modes)] + [jnp.zeros((8 - modes, nb), f32)], axis=0
    )
    modes_face = mul_exact_right(rigid_pad, one_hot[...])
    for f in range(4):
        modes_own[f] = modes_face[:, f * width:(f + 1) * width]
    mode_moves = [
        send(modes_own.at[f], modes_in.at[(f + 2) % 4], neighbours[f]) for f in range(4)
    ]

    lane_at = iota((SLOTS, lanes), 1)
    slot_at = iota((SLOTS, lanes), 0)

    loads["res"].wait()
    for move in res_moves:
        move.wait_recv()
    pieces = jnp.concatenate([res[0], res[1], -res_in[0], -res_in[1]], axis=1)
    high, low = split2(pieces)
    g_own = mul_exact_right(modes_face, repeated(high), NT)
    g_own = g_own + mul(modes_face.astype(bf16), repeated(low), NT)
    in_group = (lane_at >= slot_at * cases) & (lane_at < (slot_at + 1) * cases)
    first = jnp.sum(jnp.where(in_group, g_own, 0.0), axis=0, keepdims=True)

    def start_rows(message, own, target):
        own[...] = message
        moves = [send(own, target.at[row], at_row(s)) for s in range(1, n_row)]
        target[row] = message
        return moves

    def start_cols(message, own, target):
        own[...] = message
        moves = [send(own, target.at[col], at_col(s)) for s in range(1, n_col)]
        target[col] = message
        return moves

    def finish(moves):
        for move in moves:
            move.wait_recv()

    moves = start_rows(first, first_own, first_a)

    loads["coarse"].wait()
    finish(coarse_moves)
    patches = n_row * n_col
    span = modes * patches
    slot_c = iota((SLOTS, span), 0)
    blocks = []
    for m in range(modes):
        block = jnp.zeros((SLOTS, span), f32)
        for k in range(5):
            block = jnp.where(slot_c == k, coarse_all[k, m:m + 1, :], block)
        blocks.append(block)
    blocks.append(jnp.zeros((lanes - SLOTS * modes, span), f32))
    coarse_rows = jnp.concatenate(blocks, axis=0)
    r_at = iota((n_row, span), 0)
    q_at = iota((n_row, span), 1)
    picks = []
    for j in range(modes):
        for c in range(n_col):
            picks.append(jnp.where(q_at == (r_at * n_col + c) * modes + j, 1.0, 0.0))
    pick = jnp.concatenate(picks, axis=0).astype(bf16)
    coarse_high, coarse_low = split2(coarse_rows)
    solve_high = mul(pick, coarse_high, NT).astype(bf16)
    solve_low = mul(pick, coarse_low, NT).astype(bf16)

    finish(mode_moves)
    slot_w = iota((SLOTS, width), 0)
    columns = []
    for f in range(4):
        blocks = []
        for m in range(modes):
            block = jnp.where(slot_w == 0, modes_own[f, m:m + 1, :], 0.0)
            blocks.append(jnp.where(slot_w == 1 + f, -modes_in[f, m:m + 1, :], block))
        columns.append(jnp.concatenate(blocks, axis=0))
    basis = jnp.concatenate(columns, axis=1)
    basis_high, basis_low = split2(basis)
    rows = SLOTS * modes
    basis_both = jnp.concatenate([basis_high, basis_low], axis=0)
    basis_dof = mul(basis_both, one_hot[...], NT)
    basis_dof = basis_dof[:rows] + basis_dof[rows:]
    dof_both = jnp.concatenate(split2(basis_dof), axis=0)

    finish(moves)
    moves = start_cols(first_a[:, 0, :], first_msg, first_b)

    loads["double"].wait()
    basis_double = mul(dof_both, double[...])
    basis_double = 0.5 * basis_dof + basis_double[:rows] + basis_double[rows:]
    double_both = jnp.concatenate(split2(basis_double), axis=0)

    def contributions(vectors):
        high, low = split2(vectors)
        both = mul(dof_both, repeated(high), NT)
        return both[:rows] + both[rows:] + mul(dof_both[:rows], repeated(low), NT)

    def correction(g, columns=4 * width):
        g_t = g.T
        total = jnp.zeros((cases, lanes), f32)
        for j in range(modes):
            at = slice(j * patches, (j + 1) * patches)
            part = g_t[j * cases:(j + 1) * cases, :]
            total = total + mul_exact_right(part, solve_high[at])
            total = total + mul(part.astype(bf16), solve_low[at])
        coef = total[:, :rows]
        fix = mul_exact_right(coef, basis_high[:, :columns])
        return fix + mul(coef.astype(bf16), basis_low[:, :columns])

    def message_of(out, scalars):
        message = jnp.zeros((SLOTS, lanes), f32)
        for j in range(modes):
            mask = (lane_at >= j * cases) & (lane_at < (j + 1) * cases)
            message = jnp.where(mask, out[j * SLOTS:(j + 1) * SLOTS], message)
        lane_c = iota((cases, lanes), 1)
        case_c = iota((cases, lanes), 0)
        line = jnp.sum(
            jnp.where(lane_c == case_c + modes * cases, scalars, 0.0), axis=0, keepdims=True
        )
        return message + jnp.where(slot_at == 0, line, 0.0)

    def rolled(x, step):
        step = step % n_row
        return jnp.concatenate([x[n_row - step:], x[:n_row - step]], axis=0)

    def along_rows(buffer):
        own = buffer[:, 0, :] + rolled(buffer[:, 2, :], 1) + rolled(buffer[:, 4, :], -1)
        return jnp.stack([own, buffer[:, 1, :], buffer[:, 3, :]], axis=0)

    def along_cols(buffer):
        tiles = []
        for c in range(n_col):
            tiles.append(
                buffer[c, 0] + buffer[(c - 1) % n_col, 1] + buffer[(c + 1) % n_col, 2]
            )
        return jnp.concatenate(tiles, axis=0)

    def scalars_of(g):
        line = jnp.sum(g, axis=0, keepdims=True)
        lane_c = iota((cases, lanes), 1)
        case_c = iota((cases, lanes), 0)
        return jnp.sum(
            jnp.where(lane_c == case_c + modes * cases, line, 0.0), axis=1, keepdims=True
        )

    finish(moves)
    g = jnp.concatenate([first_b[c] for c in range(n_col)], axis=0)
    rounded_faces = (pieces - correction(g)).astype(bf16)
    rounded_full = mul(rounded_faces, one_hot[...], NT)
    rounded = rounded_full.astype(bf16)
    lifted_full = 0.5 * rounded_full + mul(rounded, double[...])
    loads["single"].wait()
    weighed_full = mul(lifted_full.astype(bf16), single[...])
    weighed = weighed_full.astype(bf16)
    weighed_full = weighed.astype(f32)
    loads["hyper"].wait()
    applied = mul(rounded, hyper[...])
    energy_parts = jnp.sum(
        rounded_full * applied + weighed_full * lifted_full, axis=1, keepdims=True
    )
    from_weighed = mul(double_both, repeated(weighed), NT)
    out = contributions(applied) + from_weighed[:rows] + from_weighed[rows:]
    moves = start_rows(message_of(out, energy_parts), own2, gather_a2)

    applied = applied + 0.5 * weighed_full + mul(weighed, double[...], NT)
    applied_faces = mul_exact_right(applied, one_hot[...])
    for f in range(4):
        faces2[f] = applied_faces[:, f * width:(f + 1) * width]
    face_moves = [
        send(faces2.at[f], faces2_in.at[(f + 2) % 4], neighbours[f]) for f in range(4)
    ]
    finish(moves)
    moves = start_cols(along_rows(gather_a2), msg2, gather_b2)

    loads["direc"].wait()
    finish(dir_moves)
    old_faces = jnp.concatenate([direc[0], direc[1], -dir_in[0], -dir_in[1]], axis=1)
    old_faces = old_faces.astype(bf16)
    loads["neumann"].wait()
    loads["eprev"].wait()
    lane_e = iota((cases, cases), 1)
    case_e = iota((cases, cases), 0)
    energy_prev = jnp.sum(
        jnp.where(lane_e == case_e, eprev[...], 0.0), axis=1, keepdims=True
    )

    finish(face_moves)
    finish(moves)
    g = along_cols(gather_b2)
    energy = scalars_of(g)
    ratio = energy / energy_prev
    jumped = applied_faces - jnp.concatenate([faces2_in[f] for f in range(4)], axis=1)
    searched = jumped - correction(g)
    paired = jnp.concatenate([searched.astype(bf16), old_faces], axis=0)
    paired = mul(paired, one_hot[...], NT)
    paired_applied = mul(paired.astype(bf16), neumann[...])
    spread_dir = paired[:cases] + ratio * paired[cases:]
    applied_dir = paired_applied[:cases] + ratio * paired_applied[cases:]
    curvature_parts = jnp.sum(spread_dir * applied_dir, axis=1, keepdims=True)
    out = contributions(applied_dir)
    moves = start_rows(message_of(out, curvature_parts), own3, gather_a3)
    dir_faces = mul_exact_right(applied_dir, one_hot[...])
    for f in range(2):
        faces3[f] = dir_faces[:, (f + 2) * width:(f + 3) * width]
    face_moves = [send(faces3.at[f], faces3_in.at[f], neighbours[f + 2]) for f in range(2)]
    finish(moves)
    moves = start_cols(along_rows(gather_a3), msg3, gather_b3)
    next_dir = [
        searched[:, f * width:(f + 1) * width] + ratio * direc[f] for f in range(2)
    ]
    for f in range(2):
        out_ref[2, f] = searched[:, f * width:(f + 1) * width]
        out_ref[3, f] = ratio * direc[f]
    finish(face_moves)
    finish(moves)
    g = along_cols(gather_b3)
    step = energy / scalars_of(g)
    fix = correction(g, 2 * width)
    for f in range(2):
        part = slice(f * width, (f + 1) * width)
        out_ref[0, f] = step * next_dir[f]
        out_ref[1, f] = step * (dir_faces[:, part] - faces3_in[f] - fix[:, part])

    for copy in sent:
        copy.wait_send()


def on_device(
    multipliers, residual, direction, energy_prev, hypersingular, double_layer,
    single_inverse, neumann_inverse, rigid_modes, coarse_inverse, face_index,
):
    n_row, n_col = lax.axis_size("row"), lax.axis_size("col")
    _, sides, cases, width = residual.shape
    modes, nb = rigid_modes.shape[1:]
    lanes = GROUPS * cases
    matrix = pltpu.VMEM((nb, nb), bf16)
    copies = 12 + 3 * (n_row + n_col - 2) + 6

    def vmem(*shape):
        return pltpu.VMEM(shape, f32)

    out = pl.pallas_call(
        functools.partial(kernel, n_row, n_col, modes),
        out_shape=jax.ShapeDtypeStruct((4, sides, cases, width), f32),
        in_specs=[pl.BlockSpec(memory_space=pltpu.HBM)] * 10,
        out_specs=pl.BlockSpec(memory_space=pltpu.VMEM),
        scratch_shapes=[
            vmem(sides, cases, width), vmem(sides, cases, width),
            vmem(1, cases), matrix, matrix, matrix, matrix,
            vmem(modes, 1, nb), pltpu.VMEM(face_index.shape[1:], jnp.int32),
            vmem(5, *coarse_inverse.shape), vmem(2, cases, width), vmem(2, cases, width),
            vmem(4, 8, width), vmem(4, 8, width), pltpu.VMEM((nb, 4 * width), bf16),
            vmem(1, lanes), vmem(n_row, 1, lanes), vmem(n_row, lanes), vmem(n_col, n_row, lanes),
            vmem(SLOTS, lanes), vmem(n_row, SLOTS, lanes),
            vmem(3, n_row, lanes), vmem(n_col, 3, n_row, lanes),
            vmem(SLOTS, lanes), vmem(n_row, SLOTS, lanes),
            vmem(3, n_row, lanes), vmem(n_col, 3, n_row, lanes),
            vmem(4, cases, width), vmem(4, cases, width),
            vmem(2, cases, width), vmem(2, cases, width),
            pltpu.SemaphoreType.DMA((10,)),
            pltpu.SemaphoreType.DMA((copies,)),
            pltpu.SemaphoreType.DMA((copies,)),
        ],
        compiler_params=pltpu.CompilerParams(
            collective_id=0, has_side_effects=True, vmem_limit_bytes=63 * 1024 * 1024
        ),
        cost_estimate=pl.CostEstimate(
            flops=40 * cases * nb * nb, bytes_accessed=8 * nb * nb, transcendentals=0
        ),
    )(
        residual[0], direction[0], energy_prev.reshape(1, cases),
        hypersingular[0], double_layer[0], single_inverse[0], neumann_inverse[0],
        rigid_modes.transpose(1, 0, 2), coarse_inverse, face_index[0],
    )
    return (multipliers + out[0], residual - out[1], (out[2] + out[3])[None])


def solution(mesh):
    split = ("row", "col")
    faces = P(split, None, None, None)
    cube = P(split, None, None)
    return jax.shard_map(
        on_device,
        mesh=mesh,
        in_specs=(
            faces, faces, faces, P(), cube, cube, cube, cube, cube, P(split, None), cube,
        ),
        out_specs=(faces, faces, faces),
        check_vma=False,
    )
```

```python
import functools

import jax
import jax.numpy as jnp
from jax import lax
from jax.experimental import pallas as pl
from jax.experimental.pallas import tpu as pltpu
from jax.sharding import PartitionSpec as P

MESH = pl.DeviceIdType.MESH
NN = (((1,), (0,)), ((), ()))
NT = (((1,), (1,)), ((), ()))
f32 = jnp.float32
bf16 = jnp.bfloat16
GROUPS = 8
SLOTS = 8


def mul(a, b, dims=NN):
    return lax.dot_general(a, b, dims, preferred_element_type=f32)


def split2(x):
    high = x.astype(bf16)
    return high, (x - high.astype(f32)).astype(bf16)


def mul_exact_right(a, b, dims=NN):
    high, low = split2(a)
    rows = a.shape[0]
    both = mul(jnp.concatenate([high, low], axis=0), b, dims)
    return both[:rows] + both[rows:]


def iota(shape, dim):
    return lax.broadcasted_iota(jnp.int32, shape, dim)


def kernel(
    n_row, n_col, modes,
    res_hbm, dir_hbm, eprev_hbm, hyper_hbm, double_hbm, single_hbm, neumann_hbm,
    rigid_hbm, coarse_hbm, face_hbm,
    out_ref,
    res, direc, eprev, hyper, double, single, neumann, rigid, face,
    coarse_all, res_in, dir_in, modes_own, modes_in, one_hot,
    own1, gathered1, own2, gathered2, own3, gathered3,
    faces2, faces2_in, faces3, faces3_in,
    local_sem, send_sem, recv_sem, gather_send_sem, gather_recv_sem,
):
    row = lax.axis_index("row")
    col = lax.axis_index("col")
    cases, width = res.shape[1], res.shape[2]
    nb = double.shape[0]
    lanes = GROUPS * cases

    def repeated(x):
        return jnp.concatenate([x] * GROUPS, axis=0)

    def at_row(s):
        return (lax.rem(row + s, n_row), col)

    def at_col(s):
        return (row, lax.rem(col + s, n_col))

    neighbours = [at_col(1), at_row(1), at_col(n_col - 1), at_row(n_row - 1)]

    loads = {}

    def load(name, src, dst):
        loads[name] = pltpu.make_async_copy(src, dst, local_sem.at[len(loads)])
        loads[name].start()

    load("face", face_hbm, face)
    load("rigid", rigid_hbm, rigid)
    load("res", res_hbm, res)
    load("coarse", coarse_hbm, coarse_all.at[0])
    load("direc", dir_hbm, direc)
    load("eprev", eprev_hbm, eprev)

    patches = n_row * n_col
    me = row * n_col + col

    def other(s):
        target = lax.rem(me + s, patches)
        return (lax.div(target, n_col), lax.rem(target, n_col))

    def each_other(body):
        def step(s, carry):
            body(s)
            return carry

        lax.fori_loop(1, patches, step, 0)

    barrier = pltpu.get_barrier_semaphore()
    each_other(
        lambda s: pl.semaphore_signal(
            barrier, inc=1, device_id=other(s), device_id_type=MESH
        )
    )
    pl.semaphore_wait(barrier, patches - 1)

    sent = []

    def send(src, dst, device):
        i = len(sent)
        copy = pltpu.make_async_remote_copy(
            src_ref=src, dst_ref=dst, send_sem=send_sem.at[i], recv_sem=recv_sem.at[i],
            device_id=device, device_id_type=MESH,
        )
        copy.start()
        sent.append(copy)
        return copy

    res_moves = [send(res_hbm.at[f], res_in.at[f], neighbours[f]) for f in range(2)]
    coarse_moves = [
        send(coarse_hbm, coarse_all.at[1 + (f + 2) % 4], neighbours[f]) for f in range(4)
    ]
    dir_moves = [send(dir_hbm.at[f], dir_in.at[f], neighbours[f]) for f in range(2)]
    load("double", double_hbm, double)
    load("single", single_hbm, single)
    load("hyper", hyper_hbm, hyper)
    load("neumann", neumann_hbm, neumann)

    loads["face"].wait()
    here = iota((nb, width), 0)
    for f in range(4):
        one_hot[:, f * width:(f + 1) * width] = jnp.where(
            here == face[f:f + 1, :], 1.0, 0.0
        ).astype(bf16)

    loads["rigid"].wait()
    rigid_pad = jnp.concatenate(
        [rigid[m] for m in range(modes)] + [jnp.zeros((8 - modes, nb), f32)], axis=0
    )
    modes_face = mul_exact_right(rigid_pad, one_hot[...])
    for f in range(4):
        modes_own[f] = modes_face[:, f * width:(f + 1) * width]
    mode_moves = [
        send(modes_own.at[f], modes_in.at[(f + 2) % 4], neighbours[f]) for f in range(4)
    ]

    lane_at = iota((SLOTS, lanes), 1)
    slot_at = iota((SLOTS, lanes), 0)

    loads["res"].wait()
    for move in res_moves:
        move.wait_recv()
    pieces = jnp.concatenate([res[0], res[1], -res_in[0], -res_in[1]], axis=1)
    high, low = split2(pieces)
    g_own = mul_exact_right(modes_face, repeated(high), NT)
    g_own = g_own + mul(modes_face.astype(bf16), repeated(low), NT)
    in_group = (lane_at >= slot_at * cases) & (lane_at < (slot_at + 1) * cases)
    first = jnp.sum(jnp.where(in_group, g_own, 0.0), axis=0, keepdims=True)

    def gather_start(message, own, gathered, parity):
        slots = gathered.shape[0]
        own[...] = message
        for k in range(slots):
            gathered[k, col, pl.ds(row, 1), :] = message[k:k + 1, :]

        def copy_of(s):
            return pltpu.make_async_remote_copy(
                src_ref=own.at[pl.ds(0, slots)],
                dst_ref=gathered.at[:, col, row, :],
                send_sem=gather_send_sem.at[s - 1],
                recv_sem=gather_recv_sem.at[parity, s - 1],
                device_id=other(s), device_id_type=MESH,
            )

        each_other(lambda s: copy_of(s).start())
        return copy_of

    def gather_finish(copy_of):
        each_other(lambda s: copy_of(s).wait())

    def finish(moves):
        for move in moves:
            move.wait_recv()

    moves = gather_start(first, own1, gathered1, 0)

    loads["coarse"].wait()
    finish(coarse_moves)
    span = modes * patches
    slot_c = iota((SLOTS, span), 0)
    blocks = []
    for m in range(modes):
        block = jnp.zeros((SLOTS, span), f32)
        for k in range(5):
            block = jnp.where(slot_c == k, coarse_all[k, m:m + 1, :], block)
        blocks.append(block)
    blocks.append(jnp.zeros((lanes - SLOTS * modes, span), f32))
    coarse_rows = jnp.concatenate(blocks, axis=0)
    r_at = iota((n_row, span), 0)
    q_at = iota((n_row, span), 1)
    picks = []
    for j in range(modes):
        for c in range(n_col):
            picks.append(jnp.where(q_at == (r_at * n_col + c) * modes + j, 1.0, 0.0))
    pick = jnp.concatenate(picks, axis=0).astype(bf16)
    coarse_high, coarse_low = split2(coarse_rows)
    solve_high = mul(pick, coarse_high, NT).astype(bf16)
    solve_low = mul(pick, coarse_low, NT).astype(bf16)

    finish(mode_moves)
    slot_w = iota((SLOTS, width), 0)
    columns = []
    for f in range(4):
        blocks = []
        for m in range(modes):
            block = jnp.where(slot_w == 0, modes_own[f, m:m + 1, :], 0.0)
            blocks.append(jnp.where(slot_w == 1 + f, -modes_in[f, m:m + 1, :], block))
        columns.append(jnp.concatenate(blocks, axis=0))
    basis = jnp.concatenate(columns, axis=1)
    basis_high, basis_low = split2(basis)
    rows = SLOTS * modes
    basis_both = jnp.concatenate([basis_high, basis_low], axis=0)
    basis_dof = mul(basis_both, one_hot[...], NT)
    basis_dof = basis_dof[:rows] + basis_dof[rows:]
    dof_both = jnp.concatenate(split2(basis_dof), axis=0)

    loads["double"].wait()
    basis_double = mul(dof_both, double[...])
    basis_double = 0.5 * basis_dof + basis_double[:rows] + basis_double[rows:]
    double_both = jnp.concatenate(split2(basis_double), axis=0)

    def contributions(vectors):
        high, low = split2(vectors)
        both = mul(dof_both, repeated(high), NT)
        return both[:rows] + both[rows:] + mul(dof_both[:rows], repeated(low), NT)

    def correction(g, columns=4 * width):
        g_t = g.T
        total = jnp.zeros((cases, lanes), f32)
        for j in range(modes):
            at = slice(j * patches, (j + 1) * patches)
            part = g_t[j * cases:(j + 1) * cases, :]
            total = total + mul_exact_right(part, solve_high[at])
            total = total + mul(part.astype(bf16), solve_low[at])
        coef = total[:, :rows]
        fix = mul_exact_right(coef, basis_high[:, :columns])
        return fix + mul(coef.astype(bf16), basis_low[:, :columns])

    def message_of(out, scalars):
        message = jnp.zeros((SLOTS, lanes), f32)
        for j in range(modes):
            mask = (lane_at >= j * cases) & (lane_at < (j + 1) * cases)
            message = jnp.where(mask, out[j * SLOTS:(j + 1) * SLOTS], message)
        lane_c = iota((cases, lanes), 1)
        case_c = iota((cases, lanes), 0)
        line = jnp.sum(
            jnp.where(lane_c == case_c + modes * cases, scalars, 0.0), axis=0, keepdims=True
        )
        return message + jnp.where(slot_at == 0, line, 0.0)

    def rolled(x, step):
        step = step % n_row
        return jnp.concatenate([x[n_row - step:], x[:n_row - step]], axis=0)

    def summed(gathered):
        tiles = []
        for c in range(n_col):
            total = gathered[0, c] + rolled(gathered[2, c], 1) + rolled(gathered[4, c], -1)
            total = total + gathered[1, (c - 1) % n_col] + gathered[3, (c + 1) % n_col]
            tiles.append(total)
        return jnp.concatenate(tiles, axis=0)

    def scalars_of(g):
        line = jnp.sum(g, axis=0, keepdims=True)
        lane_c = iota((cases, lanes), 1)
        case_c = iota((cases, lanes), 0)
        return jnp.sum(
            jnp.where(lane_c == case_c + modes * cases, line, 0.0), axis=1, keepdims=True
        )

    gather_finish(moves)
    g = jnp.concatenate([gathered1[0, c] for c in range(n_col)], axis=0)
    rounded_faces = (pieces - correction(g)).astype(bf16)
    rounded_full = mul(rounded_faces, one_hot[...], NT)
    rounded = rounded_full.astype(bf16)
    lifted_full = 0.5 * rounded_full + mul(rounded, double[...])
    loads["single"].wait()
    weighed_full = mul(lifted_full.astype(bf16), single[...])
    weighed = weighed_full.astype(bf16)
    weighed_full = weighed.astype(f32)
    loads["hyper"].wait()
    applied = mul(rounded, hyper[...])
    energy_parts = jnp.sum(
        rounded_full * applied + weighed_full * lifted_full, axis=1, keepdims=True
    )
    from_weighed = mul(double_both, repeated(weighed), NT)
    out = contributions(applied) + from_weighed[:rows] + from_weighed[rows:]
    moves = gather_start(message_of(out, energy_parts), own2, gathered2, 1)

    applied = applied + 0.5 * weighed_full + mul(weighed, double[...], NT)
    applied_faces = mul_exact_right(applied, one_hot[...])
    for f in range(4):
        faces2[f] = applied_faces[:, f * width:(f + 1) * width]
    face_moves = [
        send(faces2.at[f], faces2_in.at[(f + 2) % 4], neighbours[f]) for f in range(4)
    ]
    loads["direc"].wait()
    finish(dir_moves)
    old_faces = jnp.concatenate([direc[0], direc[1], -dir_in[0], -dir_in[1]], axis=1)
    old_faces = old_faces.astype(bf16)
    loads["neumann"].wait()
    loads["eprev"].wait()
    lane_e = iota((cases, cases), 1)
    case_e = iota((cases, cases), 0)
    energy_prev = jnp.sum(
        jnp.where(lane_e == case_e, eprev[...], 0.0), axis=1, keepdims=True
    )

    gather_finish(moves)
    g = summed(gathered2)
    energy = scalars_of(g)
    ratio = energy / energy_prev
    fix = correction(g)
    finish(face_moves)
    jumped = applied_faces - jnp.concatenate([faces2_in[f] for f in range(4)], axis=1)
    searched = jumped - fix
    paired = jnp.concatenate([searched.astype(bf16), old_faces], axis=0)
    paired = mul(paired, one_hot[...], NT)
    paired_applied = mul(paired.astype(bf16), neumann[...])
    spread_dir = paired[:cases] + ratio * paired[cases:]
    applied_dir = paired_applied[:cases] + ratio * paired_applied[cases:]
    curvature_parts = jnp.sum(spread_dir * applied_dir, axis=1, keepdims=True)
    out = contributions(applied_dir)
    moves = gather_start(message_of(out, curvature_parts), own3, gathered3, 0)
    dir_faces = mul_exact_right(applied_dir, one_hot[...])
    for f in range(2):
        faces3[f] = dir_faces[:, (f + 2) * width:(f + 3) * width]
    face_moves = [send(faces3.at[f], faces3_in.at[f], neighbours[f + 2]) for f in range(2)]
    next_dir = [
        searched[:, f * width:(f + 1) * width] + ratio * direc[f] for f in range(2)
    ]
    for f in range(2):
        out_ref[2, f] = searched[:, f * width:(f + 1) * width]
        out_ref[3, f] = ratio * direc[f]
    gather_finish(moves)
    g = summed(gathered3)
    step = energy / scalars_of(g)
    fix = correction(g, 2 * width)
    finish(face_moves)
    for f in range(2):
        part = slice(f * width, (f + 1) * width)
        out_ref[0, f] = step * next_dir[f]
        out_ref[1, f] = step * (dir_faces[:, part] - faces3_in[f] - fix[:, part])

    for copy in sent:
        copy.wait_send()


def on_device(
    multipliers, residual, direction, energy_prev, hypersingular, double_layer,
    single_inverse, neumann_inverse, rigid_modes, coarse_inverse, face_index,
):
    n_row, n_col = lax.axis_size("row"), lax.axis_size("col")
    _, sides, cases, width = residual.shape
    modes, nb = rigid_modes.shape[1:]
    lanes = GROUPS * cases
    matrix = pltpu.VMEM((nb, nb), bf16)
    copies = 18

    def vmem(*shape):
        return pltpu.VMEM(shape, f32)

    out = pl.pallas_call(
        functools.partial(kernel, n_row, n_col, modes),
        out_shape=jax.ShapeDtypeStruct((4, sides, cases, width), f32),
        in_specs=[pl.BlockSpec(memory_space=pltpu.HBM)] * 10,
        out_specs=pl.BlockSpec(memory_space=pltpu.VMEM),
        scratch_shapes=[
            vmem(sides, cases, width), vmem(sides, cases, width),
            vmem(1, cases), matrix, matrix, matrix, matrix,
            vmem(modes, 1, nb), pltpu.VMEM(face_index.shape[1:], jnp.int32),
            vmem(5, *coarse_inverse.shape), vmem(2, cases, width), vmem(2, cases, width),
            vmem(4, 8, width), vmem(4, 8, width), pltpu.VMEM((nb, 4 * width), bf16),
            vmem(1, lanes), vmem(1, n_col, n_row, lanes),
            vmem(SLOTS, lanes), vmem(5, n_col, n_row, lanes),
            vmem(SLOTS, lanes), vmem(5, n_col, n_row, lanes),
            vmem(4, cases, width), vmem(4, cases, width),
            vmem(2, cases, width), vmem(2, cases, width),
            pltpu.SemaphoreType.DMA((10,)),
            pltpu.SemaphoreType.DMA((copies,)),
            pltpu.SemaphoreType.DMA((copies,)),
            pltpu.SemaphoreType.DMA((n_row * n_col - 1,)),
            pltpu.SemaphoreType.DMA((2, n_row * n_col - 1)),
        ],
        compiler_params=pltpu.CompilerParams(
            collective_id=0, has_side_effects=True, vmem_limit_bytes=63 * 1024 * 1024
        ),
        cost_estimate=pl.CostEstimate(
            flops=40 * cases * nb * nb, bytes_accessed=8 * nb * nb, transcendentals=0
        ),
    )(
        residual[0], direction[0], energy_prev.reshape(1, cases),
        hypersingular[0], double_layer[0], single_inverse[0], neumann_inverse[0],
        rigid_modes.transpose(1, 0, 2), coarse_inverse, face_index[0],
    )
    return (multipliers + out[0], residual - out[1], (out[2] + out[3])[None])


def solution(mesh):
    split = ("row", "col")
    faces = P(split, None, None, None)
    cube = P(split, None, None)
    return jax.shard_map(
        on_device,
        mesh=mesh,
        in_specs=(
            faces, faces, faces, P(), cube, cube, cube, cube, cube, P(split, None), cube,
        ),
        out_specs=(faces, faces, faces),
        check_vma=False,
    )
```

```python
import functools

import jax
import jax.numpy as jnp
from jax import lax
from jax.experimental import pallas as pl
from jax.experimental.pallas import tpu as pltpu
from jax.sharding import PartitionSpec as P

MESH = pl.DeviceIdType.MESH
NN = (((1,), (0,)), ((), ()))
NT = (((1,), (1,)), ((), ()))
f32 = jnp.float32
bf16 = jnp.bfloat16
GROUPS = 8
SLOTS = 8


def mul(a, b, dims=NN):
    return lax.dot_general(a, b, dims, preferred_element_type=f32)


def split2(x):
    high = x.astype(bf16)
    return high, (x - high.astype(f32)).astype(bf16)


def mul_exact_right(a, b, dims=NN):
    high, low = split2(a)
    rows = a.shape[0]
    both = mul(jnp.concatenate([high, low], axis=0), b, dims)
    return both[:rows] + both[rows:]


def iota(shape, dim):
    return lax.broadcasted_iota(jnp.int32, shape, dim)


def kernel(
    n_row, n_col, modes,
    res_hbm, dir_hbm, eprev_hbm, hyper_hbm, double_hbm, single_hbm, neumann_hbm,
    rigid_hbm, coarse_hbm, face_hbm,
    out_ref,
    res, direc, eprev, hyper, double, single, neumann, rigid, face,
    coarse_all, res_in, dir_in, modes_own, modes_in, one_hot,
    own1, gathered1, own2, gathered2, own3, gathered3,
    faces2, faces2_in, faces3, faces3_in,
    local_sem, send_sem, recv_sem, gather_send_sem, gather_recv_sem,
):
    row = lax.axis_index("row")
    col = lax.axis_index("col")
    cases, width = res.shape[1], res.shape[2]
    nb = double.shape[0]
    lanes = GROUPS * cases

    def repeated(x):
        return jnp.concatenate([x] * GROUPS, axis=0)

    def at_row(s):
        return (lax.rem(row + s, n_row), col)

    def at_col(s):
        return (row, lax.rem(col + s, n_col))

    neighbours = [at_col(1), at_row(1), at_col(n_col - 1), at_row(n_row - 1)]

    loads = {}

    def load(name, src, dst):
        loads[name] = pltpu.make_async_copy(src, dst, local_sem.at[len(loads)])
        loads[name].start()

    load("face", face_hbm, face)
    load("rigid", rigid_hbm, rigid)
    load("res", res_hbm, res)
    load("coarse", coarse_hbm, coarse_all.at[0])
    load("direc", dir_hbm, direc)
    load("eprev", eprev_hbm, eprev)

    patches = n_row * n_col

    def each_other(body):
        for j in range(1, n_col):
            body(j, (row, lax.rem(col + j, n_col)))

        def step(i, carry):
            there = lax.rem(row + i, n_row)
            for j in range(n_col):
                body(i * n_col + j, (there, lax.rem(col + j, n_col)))
            return carry

        lax.fori_loop(1, n_row, step, 0)

    barrier = pltpu.get_barrier_semaphore()
    each_other(
        lambda s, device: pl.semaphore_signal(
            barrier, inc=1, device_id=device, device_id_type=MESH
        )
    )

    loads["face"].wait()
    here = iota((nb, width), 0)
    for f in range(4):
        one_hot[:, f * width:(f + 1) * width] = jnp.where(
            here == face[f:f + 1, :], 1.0, 0.0
        ).astype(bf16)
    pl.semaphore_wait(barrier, patches - 1)

    sent = []

    def send(src, dst, device):
        i = len(sent)
        copy = pltpu.make_async_remote_copy(
            src_ref=src, dst_ref=dst, send_sem=send_sem.at[i], recv_sem=recv_sem.at[i],
            device_id=device, device_id_type=MESH,
        )
        copy.start()
        sent.append(copy)
        return copy

    res_moves = [send(res_hbm.at[f], res_in.at[f], neighbours[f]) for f in range(2)]
    coarse_moves = [
        send(coarse_hbm, coarse_all.at[1 + (f + 2) % 4], neighbours[f]) for f in range(4)
    ]
    dir_moves = [send(dir_hbm.at[f], dir_in.at[f], neighbours[f]) for f in range(2)]
    load("double", double_hbm, double)
    load("single", single_hbm, single)
    load("hyper", hyper_hbm, hyper)
    load("neumann", neumann_hbm, neumann)

    loads["rigid"].wait()
    rigid_pad = jnp.concatenate(
        [rigid[m] for m in range(modes)] + [jnp.zeros((8 - modes, nb), f32)], axis=0
    )
    modes_face = mul_exact_right(rigid_pad, one_hot[...])
    for f in range(4):
        modes_own[f] = modes_face[:, f * width:(f + 1) * width]
    mode_moves = [
        send(modes_own.at[f], modes_in.at[(f + 2) % 4], neighbours[f]) for f in range(4)
    ]

    lane_at = iota((SLOTS, lanes), 1)
    slot_at = iota((SLOTS, lanes), 0)

    loads["res"].wait()
    for move in res_moves:
        move.wait_recv()
    pieces = jnp.concatenate([res[0], res[1], -res_in[0], -res_in[1]], axis=1)
    high, low = split2(pieces)
    g_own = mul_exact_right(modes_face, repeated(high), NT)
    g_own = g_own + mul(modes_face.astype(bf16), repeated(low), NT)
    in_group = (lane_at >= slot_at * cases) & (lane_at < (slot_at + 1) * cases)
    first = jnp.sum(jnp.where(in_group, g_own, 0.0), axis=0, keepdims=True)

    def gather_start(message, own, gathered, parity):
        slots = gathered.shape[0]
        own[...] = message
        for k in range(slots):
            gathered[k, col, pl.ds(row, 1), :] = message[k:k + 1, :]

        def copy_of(s, device):
            return pltpu.make_async_remote_copy(
                src_ref=own.at[pl.ds(0, slots)],
                dst_ref=gathered.at[:, col, row, :],
                send_sem=gather_send_sem.at[parity, s - 1],
                recv_sem=gather_recv_sem.at[parity, s - 1],
                device_id=device, device_id_type=MESH,
            )

        each_other(lambda s, device: copy_of(s, device).start())
        return copy_of

    def gather_finish(copy_of):
        each_other(lambda s, device: copy_of(s, device).wait_recv())

    def gather_sent(copy_of):
        each_other(lambda s, device: copy_of(s, device).wait_send())

    def finish(moves):
        for move in moves:
            move.wait_recv()

    gather1 = gather_start(first, own1, gathered1, 0)

    loads["coarse"].wait()
    finish(coarse_moves)
    span = modes * patches
    slot_c = iota((SLOTS, span), 0)
    blocks = []
    for m in range(modes):
        block = jnp.zeros((SLOTS, span), f32)
        for k in range(5):
            block = jnp.where(slot_c == k, coarse_all[k, m:m + 1, :], block)
        blocks.append(block)
    blocks.append(jnp.zeros((lanes - SLOTS * modes, span), f32))
    coarse_rows = jnp.concatenate(blocks, axis=0)
    r_at = iota((n_row, span), 0)
    q_at = iota((n_row, span), 1)
    picks = []
    for j in range(modes):
        for c in range(n_col):
            picks.append(jnp.where(q_at == (r_at * n_col + c) * modes + j, 1.0, 0.0))
    pick = jnp.concatenate(picks, axis=0).astype(bf16)
    coarse_high, coarse_low = split2(coarse_rows)
    solve_high = mul(pick, coarse_high, NT).astype(bf16)
    solve_low = mul(pick, coarse_low, NT).astype(bf16)

    finish(mode_moves)
    slot_w = iota((SLOTS, width), 0)
    columns = []
    for f in range(4):
        blocks = []
        for m in range(modes):
            block = jnp.where(slot_w == 0, modes_own[f, m:m + 1, :], 0.0)
            blocks.append(jnp.where(slot_w == 1 + f, -modes_in[f, m:m + 1, :], block))
        columns.append(jnp.concatenate(blocks, axis=0))
    basis = jnp.concatenate(columns, axis=1)
    basis_high, basis_low = split2(basis)
    rows = SLOTS * modes
    basis_both = jnp.concatenate([basis_high, basis_low], axis=0)
    basis_dof = mul(basis_both, one_hot[...], NT)
    basis_dof = basis_dof[:rows] + basis_dof[rows:]
    dof_both = jnp.concatenate(split2(basis_dof), axis=0)

    loads["double"].wait()
    basis_double = mul(dof_both, double[...])
    basis_double = 0.5 * basis_dof + basis_double[:rows] + basis_double[rows:]
    double_both = jnp.concatenate(split2(basis_double), axis=0)

    def contributions(vectors):
        high, low = split2(vectors)
        both = mul(dof_both, repeated(high), NT)
        return both[:rows] + both[rows:] + mul(dof_both[:rows], repeated(low), NT)

    def correction(g, columns=4 * width):
        g_t = g.T
        total = jnp.zeros((cases, lanes), f32)
        for j in range(modes):
            at = slice(j * patches, (j + 1) * patches)
            part = g_t[j * cases:(j + 1) * cases, :]
            total = total + mul_exact_right(part, solve_high[at])
            total = total + mul(part.astype(bf16), solve_low[at])
        coef = total[:, :rows]
        fix = mul_exact_right(coef, basis_high[:, :columns])
        return fix + mul(coef.astype(bf16), basis_low[:, :columns])

    def message_of(out, scalars):
        message = jnp.zeros((SLOTS, lanes), f32)
        for j in range(modes):
            mask = (lane_at >= j * cases) & (lane_at < (j + 1) * cases)
            message = jnp.where(mask, out[j * SLOTS:(j + 1) * SLOTS], message)
        lane_c = iota((cases, lanes), 1)
        case_c = iota((cases, lanes), 0)
        line = jnp.sum(
            jnp.where(lane_c == case_c + modes * cases, scalars, 0.0), axis=0, keepdims=True
        )
        return message + jnp.where(slot_at == 0, line, 0.0)

    def rolled(x, step):
        step = step % n_row
        return jnp.concatenate([x[n_row - step:], x[:n_row - step]], axis=0)

    def summed(gathered):
        tiles = []
        for c in range(n_col):
            total = gathered[0, c] + rolled(gathered[2, c], 1) + rolled(gathered[4, c], -1)
            total = total + gathered[1, (c - 1) % n_col] + gathered[3, (c + 1) % n_col]
            tiles.append(total)
        return jnp.concatenate(tiles, axis=0)

    def scalars_of(g):
        line = jnp.sum(g, axis=0, keepdims=True)
        lane_c = iota((cases, lanes), 1)
        case_c = iota((cases, lanes), 0)
        return jnp.sum(
            jnp.where(lane_c == case_c + modes * cases, line, 0.0), axis=1, keepdims=True
        )

    gather_finish(gather1)
    g = jnp.concatenate([gathered1[0, c] for c in range(n_col)], axis=0)
    rounded_faces = (pieces - correction(g)).astype(bf16)
    rounded_full = mul(rounded_faces, one_hot[...], NT)
    rounded = rounded_full.astype(bf16)
    lifted_full = 0.5 * rounded_full + mul(rounded, double[...])
    loads["single"].wait()
    weighed_full = mul(lifted_full.astype(bf16), single[...])
    weighed = weighed_full.astype(bf16)
    weighed_full = weighed.astype(f32)
    loads["hyper"].wait()
    applied = mul(rounded, hyper[...])
    energy_parts = jnp.sum(
        rounded_full * applied + weighed_full * lifted_full, axis=1, keepdims=True
    )
    from_weighed = mul(double_both, repeated(weighed), NT)
    out = contributions(applied) + from_weighed[:rows] + from_weighed[rows:]
    gather2 = gather_start(message_of(out, energy_parts), own2, gathered2, 1)

    applied = applied + 0.5 * weighed_full + mul(weighed, double[...], NT)
    applied_faces = mul_exact_right(applied, one_hot[...])
    for f in range(4):
        faces2[f] = applied_faces[:, f * width:(f + 1) * width]
    face_moves = [
        send(faces2.at[f], faces2_in.at[(f + 2) % 4], neighbours[f]) for f in range(4)
    ]
    loads["direc"].wait()
    finish(dir_moves)
    old_faces = jnp.concatenate([direc[0], direc[1], -dir_in[0], -dir_in[1]], axis=1)
    old_faces = old_faces.astype(bf16)
    loads["neumann"].wait()
    loads["eprev"].wait()
    lane_e = iota((cases, cases), 1)
    case_e = iota((cases, cases), 0)
    energy_prev = jnp.sum(
        jnp.where(lane_e == case_e, eprev[...], 0.0), axis=1, keepdims=True
    )

    gather_sent(gather1)
    gather_finish(gather2)
    g = summed(gathered2)
    energy = scalars_of(g)
    ratio = energy / energy_prev
    fix = correction(g)
    finish(face_moves)
    jumped = applied_faces - jnp.concatenate([faces2_in[f] for f in range(4)], axis=1)
    searched = jumped - fix
    paired = jnp.concatenate([searched.astype(bf16), old_faces], axis=0)
    paired = mul(paired, one_hot[...], NT)
    paired_applied = mul(paired.astype(bf16), neumann[...])
    spread_dir = paired[:cases] + ratio * paired[cases:]
    applied_dir = paired_applied[:cases] + ratio * paired_applied[cases:]
    curvature_parts = jnp.sum(spread_dir * applied_dir, axis=1, keepdims=True)
    out = contributions(applied_dir)
    gather3 = gather_start(message_of(out, curvature_parts), own3, gathered3, 0)
    dir_faces = mul_exact_right(applied_dir, one_hot[...])
    for f in range(2):
        faces3[f] = dir_faces[:, (f + 2) * width:(f + 3) * width]
    face_moves = [send(faces3.at[f], faces3_in.at[f], neighbours[f + 2]) for f in range(2)]
    next_dir = [
        searched[:, f * width:(f + 1) * width] + ratio * direc[f] for f in range(2)
    ]
    for f in range(2):
        out_ref[2, f] = searched[:, f * width:(f + 1) * width]
        out_ref[3, f] = ratio * direc[f]
    gather_sent(gather2)
    gather_finish(gather3)
    g = summed(gathered3)
    step = energy / scalars_of(g)
    fix = correction(g, 2 * width)
    finish(face_moves)
    for f in range(2):
        part = slice(f * width, (f + 1) * width)
        out_ref[0, f] = step * next_dir[f]
        out_ref[1, f] = step * (dir_faces[:, part] - faces3_in[f] - fix[:, part])

    gather_sent(gather3)
    for copy in sent:
        copy.wait_send()


def on_device(
    multipliers, residual, direction, energy_prev, hypersingular, double_layer,
    single_inverse, neumann_inverse, rigid_modes, coarse_inverse, face_index,
):
    n_row, n_col = lax.axis_size("row"), lax.axis_size("col")
    _, sides, cases, width = residual.shape
    modes, nb = rigid_modes.shape[1:]
    lanes = GROUPS * cases
    matrix = pltpu.VMEM((nb, nb), bf16)
    copies = 18

    def vmem(*shape):
        return pltpu.VMEM(shape, f32)

    out = pl.pallas_call(
        functools.partial(kernel, n_row, n_col, modes),
        out_shape=jax.ShapeDtypeStruct((4, sides, cases, width), f32),
        in_specs=[pl.BlockSpec(memory_space=pltpu.HBM)] * 10,
        out_specs=pl.BlockSpec(memory_space=pltpu.VMEM),
        scratch_shapes=[
            vmem(sides, cases, width), vmem(sides, cases, width),
            vmem(1, cases), matrix, matrix, matrix, matrix,
            vmem(modes, 1, nb), pltpu.VMEM(face_index.shape[1:], jnp.int32),
            vmem(5, *coarse_inverse.shape), vmem(2, cases, width), vmem(2, cases, width),
            vmem(4, 8, width), vmem(4, 8, width), pltpu.VMEM((nb, 4 * width), bf16),
            vmem(1, lanes), vmem(1, n_col, n_row, lanes),
            vmem(SLOTS, lanes), vmem(5, n_col, n_row, lanes),
            vmem(SLOTS, lanes), vmem(5, n_col, n_row, lanes),
            vmem(4, cases, width), vmem(4, cases, width),
            vmem(2, cases, width), vmem(2, cases, width),
            pltpu.SemaphoreType.DMA((10,)),
            pltpu.SemaphoreType.DMA((copies,)),
            pltpu.SemaphoreType.DMA((copies,)),
            pltpu.SemaphoreType.DMA((2, n_row * n_col - 1)),
            pltpu.SemaphoreType.DMA((2, n_row * n_col - 1)),
        ],
        compiler_params=pltpu.CompilerParams(
            collective_id=0, has_side_effects=True, vmem_limit_bytes=63 * 1024 * 1024
        ),
        cost_estimate=pl.CostEstimate(
            flops=40 * cases * nb * nb, bytes_accessed=8 * nb * nb, transcendentals=0
        ),
    )(
        residual[0], direction[0], energy_prev.reshape(1, cases),
        hypersingular[0], double_layer[0], single_inverse[0], neumann_inverse[0],
        rigid_modes.transpose(1, 0, 2), coarse_inverse, face_index[0],
    )
    return (multipliers + out[0], residual - out[1], (out[2] + out[3])[None])


def solution(mesh):
    split = ("row", "col")
    faces = P(split, None, None, None)
    cube = P(split, None, None)
    return jax.shard_map(
        on_device,
        mesh=mesh,
        in_specs=(
            faces, faces, faces, P(), cube, cube, cube, cube, cube, P(split, None), cube,
        ),
        out_specs=(faces, faces, faces),
        check_vma=False,
    )
```

```python
import functools

import jax
import jax.numpy as jnp
from jax import lax
from jax.experimental import pallas as pl
from jax.experimental.pallas import tpu as pltpu
from jax.sharding import PartitionSpec as P

MESH = pl.DeviceIdType.MESH
NN = (((1,), (0,)), ((), ()))
NT = (((1,), (1,)), ((), ()))
f32 = jnp.float32
bf16 = jnp.bfloat16
GROUPS = 8
SLOTS = 8


def mul(a, b, dims=NN):
    return lax.dot_general(a, b, dims, preferred_element_type=f32)


def split2(x):
    high = x.astype(bf16)
    return high, (x - high.astype(f32)).astype(bf16)


def mul_exact_right(a, b, dims=NN):
    high, low = split2(a)
    rows = a.shape[0]
    both = mul(jnp.concatenate([high, low], axis=0), b, dims)
    return both[:rows] + both[rows:]


def iota(shape, dim):
    return lax.broadcasted_iota(jnp.int32, shape, dim)


def kernel(
    n_row, n_col, modes,
    res_hbm, dir_hbm, eprev_hbm, hyper_hbm, double_hbm, single_hbm, neumann_hbm,
    rigid_hbm, coarse_hbm, face_hbm,
    out_ref,
    res, direc, eprev, hyper, double, single, neumann, rigid, face,
    coarse_all, res_in, dir_in, modes_own, modes_in, one_hot, one_hot_t,
    own1, gathered1, own2, gathered2, own3, gathered3,
    faces2, faces2_in, faces3, faces3_in,
    local_sem, send_sem, recv_sem, gather_send_sem, gather_recv_sem,
):
    row = lax.axis_index("row")
    col = lax.axis_index("col")
    cases, width = res.shape[1], res.shape[2]
    nb = double.shape[0]
    lanes = GROUPS * cases

    def repeated(x):
        return jnp.concatenate([x] * GROUPS, axis=0)

    def at_row(s):
        return (lax.rem(row + s, n_row), col)

    def at_col(s):
        return (row, lax.rem(col + s, n_col))

    neighbours = [at_col(1), at_row(1), at_col(n_col - 1), at_row(n_row - 1)]

    loads = {}

    def load(name, src, dst):
        loads[name] = pltpu.make_async_copy(src, dst, local_sem.at[len(loads)])
        loads[name].start()

    load("face", face_hbm, face)
    load("rigid", rigid_hbm, rigid)
    load("res", res_hbm, res)
    load("coarse", coarse_hbm, coarse_all.at[0])
    load("direc", dir_hbm, direc)
    load("eprev", eprev_hbm, eprev)

    patches = n_row * n_col
    me = row * n_col + col

    def other(s):
        target = lax.rem(me + s, patches)
        return (lax.div(target, n_col), lax.rem(target, n_col))

    def each_other(body):
        def step(s, carry):
            body(s)
            return carry

        lax.fori_loop(1, patches, step, 0)

    barrier = pltpu.get_barrier_semaphore()
    each_other(
        lambda s: pl.semaphore_signal(
            barrier, inc=1, device_id=other(s), device_id_type=MESH
        )
    )
    pl.semaphore_wait(barrier, patches - 1)

    sent = []

    def send(src, dst, device):
        i = len(sent)
        copy = pltpu.make_async_remote_copy(
            src_ref=src, dst_ref=dst, send_sem=send_sem.at[i], recv_sem=recv_sem.at[i],
            device_id=device, device_id_type=MESH,
        )
        copy.start()
        sent.append(copy)
        return copy

    res_moves = [send(res_hbm.at[f], res_in.at[f], neighbours[f]) for f in range(2)]
    coarse_moves = [
        send(coarse_hbm, coarse_all.at[1 + (f + 2) % 4], neighbours[f]) for f in range(4)
    ]
    dir_moves = [send(dir_hbm.at[f], dir_in.at[f], neighbours[f]) for f in range(2)]
    load("double", double_hbm, double)
    load("single", single_hbm, single)
    load("hyper", hyper_hbm, hyper)
    load("neumann", neumann_hbm, neumann)

    loads["face"].wait()
    here = iota((nb, width), 0)
    for f in range(4):
        one_hot[:, f * width:(f + 1) * width] = jnp.where(
            here == face[f:f + 1, :], 1.0, 0.0
        ).astype(bf16)

    loads["rigid"].wait()
    rigid_pad = jnp.concatenate(
        [rigid[m] for m in range(modes)] + [jnp.zeros((8 - modes, nb), f32)], axis=0
    )
    modes_face = mul_exact_right(rigid_pad, one_hot[...])
    for f in range(4):
        modes_own[f] = modes_face[:, f * width:(f + 1) * width]
    mode_moves = [
        send(modes_own.at[f], modes_in.at[(f + 2) % 4], neighbours[f]) for f in range(4)
    ]

    lane_at = iota((SLOTS, lanes), 1)
    slot_at = iota((SLOTS, lanes), 0)

    loads["res"].wait()
    for move in res_moves:
        move.wait_recv()
    pieces = jnp.concatenate([res[0], res[1], -res_in[0], -res_in[1]], axis=1)
    high, low = split2(pieces)
    g_own = mul_exact_right(modes_face, repeated(high), NT)
    g_own = g_own + mul(modes_face.astype(bf16), repeated(low), NT)
    in_group = (lane_at >= slot_at * cases) & (lane_at < (slot_at + 1) * cases)
    first = jnp.sum(jnp.where(in_group, g_own, 0.0), axis=0, keepdims=True)

    def gather_start(message, own, gathered, parity):
        slots = gathered.shape[0]
        own[...] = message
        for k in range(slots):
            gathered[k, col, pl.ds(row, 1), :] = message[k:k + 1, :]

        def copy_of(s):
            return pltpu.make_async_remote_copy(
                src_ref=own.at[pl.ds(0, slots)],
                dst_ref=gathered.at[:, col, row, :],
                send_sem=gather_send_sem.at[s - 1],
                recv_sem=gather_recv_sem.at[parity, s - 1],
                device_id=other(s), device_id_type=MESH,
            )

        each_other(lambda s: copy_of(s).start())
        return copy_of

    def gather_finish(copy_of):
        each_other(lambda s: copy_of(s).wait())

    def finish(moves):
        for move in moves:
            move.wait_recv()

    moves = gather_start(first, own1, gathered1, 0)

    face_rows = face[...].astype(f32)
    face_columns = jnp.concatenate([face_rows, jnp.zeros((4, width), f32)], axis=0).T
    there = iota((width, nb), 1).astype(f32)
    for f in range(4):
        one_hot_t[f * width:(f + 1) * width, :] = jnp.where(
            there == face_columns[:, f:f + 1], 1.0, 0.0
        ).astype(bf16)

    loads["coarse"].wait()
    finish(coarse_moves)
    span = modes * patches
    slot_c = iota((SLOTS, span), 0)
    blocks = []
    for m in range(modes):
        block = jnp.zeros((SLOTS, span), f32)
        for k in range(5):
            block = jnp.where(slot_c == k, coarse_all[k, m:m + 1, :], block)
        blocks.append(block)
    blocks.append(jnp.zeros((lanes - SLOTS * modes, span), f32))
    coarse_rows = jnp.concatenate(blocks, axis=0)
    r_at = iota((n_row, span), 0)
    q_at = iota((n_row, span), 1)
    picks = []
    for j in range(modes):
        for c in range(n_col):
            picks.append(jnp.where(q_at == (r_at * n_col + c) * modes + j, 1.0, 0.0))
    pick = jnp.concatenate(picks, axis=0).astype(bf16)
    coarse_high, coarse_low = split2(coarse_rows)
    solve_high = mul(pick, coarse_high, NT).astype(bf16)
    solve_low = mul(pick, coarse_low, NT).astype(bf16)

    finish(mode_moves)
    slot_w = iota((SLOTS, width), 0)
    columns = []
    for f in range(4):
        blocks = []
        for m in range(modes):
            block = jnp.where(slot_w == 0, modes_own[f, m:m + 1, :], 0.0)
            blocks.append(jnp.where(slot_w == 1 + f, -modes_in[f, m:m + 1, :], block))
        columns.append(jnp.concatenate(blocks, axis=0))
    basis = jnp.concatenate(columns, axis=1)
    basis_high, basis_low = split2(basis)
    rows = SLOTS * modes
    basis_both = jnp.concatenate([basis_high, basis_low], axis=0)
    basis_dof = mul(basis_both, one_hot_t[...])
    basis_dof = basis_dof[:rows] + basis_dof[rows:]
    dof_both = jnp.concatenate(split2(basis_dof), axis=0)

    loads["double"].wait()
    basis_double = mul(dof_both, double[...])
    basis_double = 0.5 * basis_dof + basis_double[:rows] + basis_double[rows:]
    double_both = jnp.concatenate(split2(basis_double), axis=0)

    def contributions(vectors):
        high, low = split2(vectors)
        both = mul(dof_both, repeated(high), NT)
        return both[:rows] + both[rows:] + mul(dof_both[:rows], repeated(low), NT)

    def correction(g, columns=4 * width):
        g_t = g.T
        total = jnp.zeros((cases, lanes), f32)
        for j in range(modes):
            at = slice(j * patches, (j + 1) * patches)
            part = g_t[j * cases:(j + 1) * cases, :]
            total = total + mul_exact_right(part, solve_high[at])
            total = total + mul(part.astype(bf16), solve_low[at])
        coef = total[:, :rows]
        fix = mul_exact_right(coef, basis_high[:, :columns])
        return fix + mul(coef.astype(bf16), basis_low[:, :columns])

    def message_of(out, scalars):
        message = jnp.zeros((SLOTS, lanes), f32)
        for j in range(modes):
            mask = (lane_at >= j * cases) & (lane_at < (j + 1) * cases)
            message = jnp.where(mask, out[j * SLOTS:(j + 1) * SLOTS], message)
        lane_c = iota((cases, lanes), 1)
        case_c = iota((cases, lanes), 0)
        line = jnp.sum(
            jnp.where(lane_c == case_c + modes * cases, scalars, 0.0), axis=0, keepdims=True
        )
        return message + jnp.where(slot_at == 0, line, 0.0)

    def rolled(x, step):
        step = step % n_row
        return jnp.concatenate([x[n_row - step:], x[:n_row - step]], axis=0)

    def summed(gathered):
        tiles = []
        for c in range(n_col):
            total = gathered[0, c] + rolled(gathered[2, c], 1) + rolled(gathered[4, c], -1)
            total = total + gathered[1, (c - 1) % n_col] + gathered[3, (c + 1) % n_col]
            tiles.append(total)
        return jnp.concatenate(tiles, axis=0)

    def scalars_of(g):
        line = jnp.sum(g, axis=0, keepdims=True)
        lane_c = iota((cases, lanes), 1)
        case_c = iota((cases, lanes), 0)
        return jnp.sum(
            jnp.where(lane_c == case_c + modes * cases, line, 0.0), axis=1, keepdims=True
        )

    gather_finish(moves)
    g = jnp.concatenate([gathered1[0, c] for c in range(n_col)], axis=0)
    rounded_faces = (pieces - correction(g)).astype(bf16)
    rounded_full = mul(rounded_faces, one_hot_t[...])
    rounded = rounded_full.astype(bf16)
    lifted_full = 0.5 * rounded_full + mul(rounded, double[...])
    loads["single"].wait()
    weighed_full = mul(lifted_full.astype(bf16), single[...])
    weighed = weighed_full.astype(bf16)
    weighed_full = weighed.astype(f32)
    loads["hyper"].wait()
    applied = mul(rounded, hyper[...])
    energy_parts = jnp.sum(
        rounded_full * applied + weighed_full * lifted_full, axis=1, keepdims=True
    )
    from_weighed = mul(double_both, repeated(weighed), NT)
    out = contributions(applied) + from_weighed[:rows] + from_weighed[rows:]
    moves = gather_start(message_of(out, energy_parts), own2, gathered2, 1)

    applied = applied + 0.5 * weighed_full + mul(weighed, double[...], NT)
    applied_faces = mul_exact_right(applied, one_hot[...])
    for f in range(4):
        faces2[f] = applied_faces[:, f * width:(f + 1) * width]
    face_moves = [
        send(faces2.at[f], faces2_in.at[(f + 2) % 4], neighbours[f]) for f in range(4)
    ]
    loads["direc"].wait()
    finish(dir_moves)
    old_faces = jnp.concatenate([direc[0], direc[1], -dir_in[0], -dir_in[1]], axis=1)
    old_faces = old_faces.astype(bf16)
    loads["neumann"].wait()
    loads["eprev"].wait()
    lane_e = iota((cases, cases), 1)
    case_e = iota((cases, cases), 0)
    energy_prev = jnp.sum(
        jnp.where(lane_e == case_e, eprev[...], 0.0), axis=1, keepdims=True
    )

    gather_finish(moves)
    g = summed(gathered2)
    energy = scalars_of(g)
    ratio = energy / energy_prev
    fix = correction(g)
    finish(face_moves)
    jumped = applied_faces - jnp.concatenate([faces2_in[f] for f in range(4)], axis=1)
    searched = jumped - fix
    paired = jnp.concatenate([searched.astype(bf16), old_faces], axis=0)
    paired = mul(paired, one_hot_t[...])
    paired_applied = mul(paired.astype(bf16), neumann[...])
    spread_dir = paired[:cases] + ratio * paired[cases:]
    applied_dir = paired_applied[:cases] + ratio * paired_applied[cases:]
    curvature_parts = jnp.sum(spread_dir * applied_dir, axis=1, keepdims=True)
    out = contributions(applied_dir)
    moves = gather_start(message_of(out, curvature_parts), own3, gathered3, 0)
    dir_faces = mul_exact_right(applied_dir, one_hot[...])
    for f in range(2):
        faces3[f] = dir_faces[:, (f + 2) * width:(f + 3) * width]
    face_moves = [send(faces3.at[f], faces3_in.at[f], neighbours[f + 2]) for f in range(2)]
    next_dir = [
        searched[:, f * width:(f + 1) * width] + ratio * direc[f] for f in range(2)
    ]
    for f in range(2):
        out_ref[2, f] = searched[:, f * width:(f + 1) * width]
        out_ref[3, f] = ratio * direc[f]
    gather_finish(moves)
    g = summed(gathered3)
    step = energy / scalars_of(g)
    fix = correction(g, 2 * width)
    finish(face_moves)
    for f in range(2):
        part = slice(f * width, (f + 1) * width)
        out_ref[0, f] = step * next_dir[f]
        out_ref[1, f] = step * (dir_faces[:, part] - faces3_in[f] - fix[:, part])

    for copy in sent:
        copy.wait_send()


def on_device(
    multipliers, residual, direction, energy_prev, hypersingular, double_layer,
    single_inverse, neumann_inverse, rigid_modes, coarse_inverse, face_index,
):
    n_row, n_col = lax.axis_size("row"), lax.axis_size("col")
    _, sides, cases, width = residual.shape
    modes, nb = rigid_modes.shape[1:]
    lanes = GROUPS * cases
    matrix = pltpu.VMEM((nb, nb), bf16)
    copies = 18

    def vmem(*shape):
        return pltpu.VMEM(shape, f32)

    out = pl.pallas_call(
        functools.partial(kernel, n_row, n_col, modes),
        out_shape=jax.ShapeDtypeStruct((4, sides, cases, width), f32),
        in_specs=[pl.BlockSpec(memory_space=pltpu.HBM)] * 10,
        out_specs=pl.BlockSpec(memory_space=pltpu.VMEM),
        scratch_shapes=[
            vmem(sides, cases, width), vmem(sides, cases, width),
            vmem(1, cases), matrix, matrix, matrix, matrix,
            vmem(modes, 1, nb), pltpu.VMEM(face_index.shape[1:], jnp.int32),
            vmem(5, *coarse_inverse.shape), vmem(2, cases, width), vmem(2, cases, width),
            vmem(4, 8, width), vmem(4, 8, width), pltpu.VMEM((nb, 4 * width), bf16),
            pltpu.VMEM((4 * width, nb), bf16),
            vmem(1, lanes), vmem(1, n_col, n_row, lanes),
            vmem(SLOTS, lanes), vmem(5, n_col, n_row, lanes),
            vmem(SLOTS, lanes), vmem(5, n_col, n_row, lanes),
            vmem(4, cases, width), vmem(4, cases, width),
            vmem(2, cases, width), vmem(2, cases, width),
            pltpu.SemaphoreType.DMA((10,)),
            pltpu.SemaphoreType.DMA((copies,)),
            pltpu.SemaphoreType.DMA((copies,)),
            pltpu.SemaphoreType.DMA((n_row * n_col - 1,)),
            pltpu.SemaphoreType.DMA((2, n_row * n_col - 1)),
        ],
        compiler_params=pltpu.CompilerParams(
            collective_id=0, has_side_effects=True, vmem_limit_bytes=63 * 1024 * 1024
        ),
        cost_estimate=pl.CostEstimate(
            flops=40 * cases * nb * nb, bytes_accessed=8 * nb * nb, transcendentals=0
        ),
    )(
        residual[0], direction[0], energy_prev.reshape(1, cases),
        hypersingular[0], double_layer[0], single_inverse[0], neumann_inverse[0],
        rigid_modes.transpose(1, 0, 2), coarse_inverse, face_index[0],
    )
    return (multipliers + out[0], residual - out[1], (out[2] + out[3])[None])


def solution(mesh):
    split = ("row", "col")
    faces = P(split, None, None, None)
    cube = P(split, None, None)
    return jax.shard_map(
        on_device,
        mesh=mesh,
        in_specs=(
            faces, faces, faces, P(), cube, cube, cube, cube, cube, P(split, None), cube,
        ),
        out_specs=(faces, faces, faces),
        check_vma=False,
    )
```
